256 devices in a mesh: gx: 16 (over x, y), gy: 8 (over z), ta: 2 (over core).
Axes of the slice: x: 4, y: 4, z: 8, core: 2. Of those that a mesh axis runs over, the one named last changes fastest.
Arguments:
- movie: bfloat16 [16, 8, 128, 32, 1024], P('gx', 'gy', None, 'ta'), may hold values from -4 to 6
- pieces: bfloat16 [16, 8, 128, 16, 1024], P('gx', 'gy'), may hold values from 0 to 0.053955078
- owner: int32 [16, 8, 2048, 1], P('gx', 'gy'), may hold values from 0 to 127; in each aligned block of 2048 rows (0 to 2047, 2048 to 4095, ..., all dimensions but the last counted through in order) at most 64 rows name the same one
- block_offset: int32 [16, 8, 2048], P('gx', 'gy'), may hold values from 0 to 1023
- light: bfloat16 [16, 8, 128, 1024], P('gx', 'gy'), may hold values from 0.3 to 6.5, as said below
- traces: float32 [32, 131072], P('ta', ('gx', 'gy')), may hold values from 0 to 2
- ar_first: float32 [131072], P(('gx', 'gy')), may hold values from 0.8 to 1.4
- ar_second: float32 [131072], P(('gx', 'gy')), may hold values from -0.45 to -0.05
- mixing: bfloat16 [32, 32, 131072], P(None, None, ('gx', 'gy')), may hold values from -0.13 to 0.43
Outputs:
- traces_out: float32 [32, 131072], P('ta', ('gx', 'gy'))
- background: float32 [32], P('ta')
The draws below stay inside these ranges and needn't reach their ends.
Inputs may be any that keep to these rules, and one draw needn't show every extreme that they name: At most 64 slots of one tile name the same owner, and some tile has exactly 64 slots for one owner. `light`: Positive.
All inputs are finite; a program needn't handle non-finite values.
Results may differ from the reference program's by a relative error of at most 0.011.
Values may be sent and summed in bfloat16 or wider, within the bound.
A program may use at most 64 MiB of HBM per device.

```python
import math
import jax
import jax.numpy as jnp
import numpy as np
from jax import lax

PIX = 1024
CELLS = 128
PER = 16
FRAMES = 32
OWN = 1024
DECONV_ITERS = 3
PASSES = 2
CAP = 64
NEUR = 131072
N_GX = 16
N_GY = 8


def draw_movie(key, part):
    key = jax.random.fold_in(key, 11)
    shape = (N_GX, N_GY, CELLS, FRAMES, PIX)
    noise = jnp.clip(jax.random.normal(key, shape, jnp.float32), -5.0, 5.0)
    return (noise + 1.0).astype(jnp.bfloat16)


def draw_light(key, part):
    key = jax.random.fold_in(key, 23)
    shape = (N_GX, N_GY, CELLS, PIX)
    row_place = lax.broadcasted_iota(jnp.float32, shape, 0) / max(N_GX - 1, 1)
    col_place = lax.broadcasted_iota(jnp.float32, shape, 1) / max(N_GY - 1, 1)
    profile = (1.0 + 2.0 * row_place) * (1.0 + col_place)
    factor = jax.random.uniform(key, shape, jnp.float32, 0.3, 1.0)
    return (profile * factor).astype(jnp.bfloat16)


def draw_mixing(key, part):
    key = jax.random.fold_in(key, 37)
    shape = (FRAMES, FRAMES, NEUR)
    later = lax.broadcasted_iota(jnp.float32, shape, 0)
    earlier = lax.broadcasted_iota(jnp.float32, shape, 1)
    spacing = jnp.abs(later - earlier)
    spread = jax.random.uniform(key, shape, jnp.float32, -1.0, 1.0)
    diagonal_part = jnp.where(spacing == 0.0, 0.3, 0.0)
    return (diagonal_part + 0.12 * spread * jnp.power(0.8, spacing)).astype(jnp.bfloat16)


def place_ends(array, stream_key, smallest, top_value):
    longest = array.shape.index(max(array.shape))
    spots = []
    for shift in (0, 1):
        where = [jax.random.randint(jax.random.fold_in(stream_key, axis), (), 0, length) for axis, length in enumerate(array.shape)]
        where[longest] = (where[longest] + shift) % array.shape[longest]
        spots.append(tuple(where))
    return array.at[spots[0]].set(smallest).at[spots[1]].set(top_value)


def block_levels(key, dims, split, least, high):
    level, own = 1.0, jax.random.fold_in(key, 6)
    for dim, parts in split:
        steps = jnp.exp(jax.random.uniform(jax.random.fold_in(own, dim), (parts,), jnp.float32, least / len(split), high / len(split)))
        level = level * jnp.repeat(steps, dims[dim] // parts).reshape([-1 if axis == dim else 1 for axis in range(len(dims))])
    return level


def assign_block(stream_key, own, number, rows, number_of, top, limit, slope):
    sequence = jax.random.permutation(stream_key, number_of)
    crowded, usual = portions_of(number_of, rows * top, limit, slope, True), portions_of(number_of, rows * top, limit, slope, False)
    places = jnp.arange(number_of)

    def named(lengths, rotation):
        used = int((lengths > 0).sum())
        fixed = max(1, used // 4)
        passed = fixed + (places - fixed + rotation * (used - fixed)) % max(1, number_of - fixed)
        return jnp.zeros((number_of,), jnp.int32).at[sequence[jnp.where(places < fixed, places, passed)]].set(jnp.asarray(lengths, jnp.int32))

    lengths = jnp.where(number % 4 == 0, named(crowded, number // 4), named(usual, number - number // 4 - 1))
    mixed = jax.random.permutation(jax.random.fold_in(own, 3), number_of)
    source_of, taker = mixed[0:number_of // 2 * 2:2], mixed[1:number_of // 2 * 2:2]
    slack = jnp.minimum(lengths[source_of] - 1, limit - lengths[taker]) // 2
    slack = jnp.where((source_of == sequence[0]) | (taker == sequence[0]) | (lengths[taker] == 0), 0, jnp.maximum(slack, 0))
    passed = jax.random.randint(jax.random.fold_in(own, 4), (number_of // 2,), 0, 1 << 20) % (slack + 1)
    lengths = lengths.at[source_of].add(-passed).at[taker].add(passed)
    items = jnp.searchsorted(jnp.cumsum(lengths), jnp.arange(rows * top), side="right").astype(jnp.int32)
    grid = items.reshape(top, rows).T
    grid = grid[jax.random.permutation(jax.random.fold_in(own, 1), rows)]
    rotation = jax.random.randint(jax.random.fold_in(own, 2), (rows, 1), 0, top)
    return jnp.take_along_axis(grid, (jnp.arange(top)[None, :] + rotation) % top, axis=1)


def portions_of(number_of, total, bound, lean, full):
    loads = [(1 << 20) // math.isqrt(rank ** lean) + 1 for rank in range(1, number_of + 1)]
    largest = bound if full else min(bound, max(-(-total // number_of), total * loads[0] // sum(loads)))
    least = 1 if total - largest >= number_of - 1 else 0
    given, rest = [largest] + [least] * (number_of - 1), total - largest - least * (number_of - 1)
    while rest > 0:
        movable = [i for i in range(1, number_of) if given[i] < largest] or [i for i in range(1, number_of) if given[i] < bound]
        pool, budget = sum([loads[i] for i in movable]), rest
        for i in movable:
            more = min(bound - given[i], max(1, budget * loads[i] // pool), rest)
            given[i] = given[i] + more
            rest = rest - more
    return np.array(given)


def setup_inputs(seed: int = 0) -> dict:
    key_list = jax.random.split(jax.random.key(seed), 10)
    movie = draw_movie(jax.random.fold_in(key_list[9], 71), 0)
    pieces = jnp.clip(0.053955078 * jax.random.uniform(key_list[1], (N_GX, N_GY, CELLS, PER, PIX), jnp.float32) ** block_levels(key_list[1], (N_GX, N_GY, CELLS, PER, PIX), ((0, 16), (1, 8)), -0.2, 0.2), 0.0, 0.053955078).astype(jnp.bfloat16)
    owner_keys = jax.random.split(jax.random.fold_in(key_list[2], 1), N_GX * N_GY * (CELLS * PER) // (CELLS * PER))
    owner_turns = jax.random.permutation(jax.random.fold_in(key_list[2], 3), N_GX * N_GY * (CELLS * PER) // (CELLS * PER))
    owner = jax.vmap(lambda own, number: assign_block(jax.random.fold_in(key_list[2], 2), own, number, CELLS * PER, N_GX * N_GY, 1, CAP, 2))(owner_keys, owner_turns).reshape((N_GX, N_GY, CELLS * PER, 1))
    block_offset = place_ends(jax.random.randint(key_list[3], (N_GX, N_GY, CELLS * PER), 0, OWN), jax.random.fold_in(key_list[3], 1), 0, OWN - 1).astype(jnp.int32)
    light = draw_light(jax.random.fold_in(key_list[9], 71), 0)
    traces = jnp.clip(2.0 * jax.random.uniform(key_list[5], (FRAMES, NEUR), jnp.float32) ** block_levels(key_list[5], (FRAMES, NEUR), ((0, 2), (1, 128)), -0.2, 0.2), 0.0, 2.0)
    ar_first = jnp.clip(0.8 + 0.59999996 * jax.random.uniform(key_list[6], (NEUR,), jnp.float32) ** block_levels(key_list[6], (NEUR,), ((0, 128),), -0.2, 0.2), 0.8, 1.4)
    ar_second = jnp.clip(-0.45 + 0.39999999 * jax.random.uniform(key_list[7], (NEUR,), jnp.float32) ** block_levels(key_list[7], (NEUR,), ((0, 128),), -0.2, 0.2), -0.45, -0.05)
    mixing = draw_mixing(jax.random.fold_in(key_list[9], 71), 0)
    return {"movie": movie, "pieces": pieces, "owner": owner, "block_offset": block_offset, "light": light, "traces": traces, "ar_first": ar_first, "ar_second": ar_second, "mixing": mixing}


def forward_filter(values, first_lag, second_lag):
    prev_one = jnp.concatenate([jnp.zeros_like(values[:1]), values[:-1]], 0)
    prev_two = jnp.concatenate([jnp.zeros_like(values[:2]), values[:-2]], 0)
    return values - first_lag * prev_one - second_lag * prev_two


def adjoint_filter(values, first_lag, second_lag):
    next_one = jnp.concatenate([values[1:], jnp.zeros_like(values[:1])], 0)
    next_two = jnp.concatenate([values[2:], jnp.zeros_like(values[:2])], 0)
    return values - first_lag * next_one - second_lag * next_two


def deconvolve(target, first_lag, second_lag, inverse_block):
    inverse_wide = inverse_block.astype(jnp.float32)
    latest = target
    scaled_dual = jnp.zeros_like(target)
    for sweep in range(DECONV_ITERS):
        filtered = forward_filter(latest, first_lag, second_lag)
        spikes = jnp.maximum(filtered + scaled_dual, 0.0)
        scaled_dual = scaled_dual + filtered - spikes
        driven = target + adjoint_filter(spikes - scaled_dual, first_lag, second_lag)
        latest = jnp.sum(inverse_wide * driven[None, :, :], axis=1)
    return latest


def reference(movie, pieces, owner, block_offset, light, traces, ar_first, ar_second, mixing):
    tile_count = N_GX * N_GY
    slot_count = CELLS * PER
    neuron_index = (owner[..., 0] * OWN + block_offset).reshape(-1).astype(jnp.int32)
    tile_movie = movie.reshape(tile_count, CELLS, FRAMES, PIX)
    tile_pieces = pieces.reshape(tile_count, CELLS, PER, PIX)
    tile_light = light.reshape(tile_count, CELLS, PIX)

    def piece_energy(piece_block):
        wide = piece_block.astype(jnp.float32)
        return jnp.sum(wide * wide, -1).reshape(slot_count)

    piece_norm = lax.map(piece_energy, tile_pieces).reshape(-1)
    light_wide = light.astype(jnp.float32)
    energy = jnp.sum(light_wide * light_wide)
    weight = jnp.zeros((NEUR,), jnp.float32).at[neuron_index].add(piece_norm)
    lag_one = ar_first.reshape(tile_count, OWN)
    lag_two = ar_second.reshape(tile_count, OWN)
    inverse_blocks = jnp.moveaxis(mixing.reshape(FRAMES, FRAMES, tile_count, OWN), 2, 0)
    current = traces
    background = jnp.zeros((FRAMES,), jnp.float32)
    for pass_index in range(PASSES):
        copies = jnp.take(current, neuron_index, axis=1).astype(jnp.bfloat16)
        copies = jnp.moveaxis(copies.reshape(FRAMES, tile_count, CELLS, PER), 1, 0)

        def error_of(packed):
            movie_block, piece_block, copy_block = packed
            modeled = jnp.einsum("ckp,fck->cfp", piece_block.astype(jnp.float32), copy_block.astype(jnp.float32))
            return movie_block.astype(jnp.float32) - modeled

        def light_numerator(packed):
            error = error_of(packed[:3])
            light_block = packed[3].astype(jnp.float32)
            return jnp.sum(light_block[:, None, :] * error, axis=(0, 2))

        numerators = lax.map(light_numerator, (tile_movie, tile_pieces, copies, tile_light))
        background = jnp.sum(numerators, 0) / (energy + 1e-6)

        def trace_partials(packed):
            error = error_of(packed[:3])
            light_block = packed[3].astype(jnp.float32)
            residual = (error - light_block[:, None, :] * background[None, :, None]).astype(jnp.bfloat16)
            partial_block = jnp.einsum("ckp,cfp->fck", packed[1].astype(jnp.float32), residual.astype(jnp.float32))
            return partial_block.reshape(FRAMES, slot_count)

        partials = lax.map(trace_partials, (tile_movie, tile_pieces, copies, tile_light))
        flat = jnp.moveaxis(partials, 0, 1).reshape(FRAMES, tile_count * slot_count)
        summed = jnp.zeros((FRAMES, NEUR), jnp.float32).at[:, neuron_index].add(flat)
        estimate = current + summed / jnp.maximum(weight, 1.0)
        blocks = jnp.moveaxis(estimate.reshape(FRAMES, tile_count, OWN), 1, 0)

        def clean_block(packed):
            return deconvolve(packed[0], packed[1], packed[2], packed[3])

        cleaned = lax.map(clean_block, (blocks, lag_one, lag_two, inverse_blocks))
        current = jnp.moveaxis(cleaned, 0, 1).reshape(FRAMES, NEUR)
    return current, background
```

```python
import functools
import math

import jax
import jax.numpy as jnp
from jax import lax
from jax.experimental import pallas as pl
from jax.experimental.pallas import tpu as pltpu
from jax.sharding import PartitionSpec as P

DECONV_ITERS = 3
PASSES = 2
CAP = 64
MESH = pl.DeviceIdType.MESH
F32, BF16, I32 = jnp.float32, jnp.bfloat16, jnp.int32


def iota(shape, axis):
    return lax.broadcasted_iota(I32, shape, axis)


def dot(left, right):
    return lax.dot_general(left, right, (((1,), (0,)), ((), ())), preferred_element_type=F32)


def dot_t(left, right):
    return lax.dot_general(left, right, (((1,), (1,)), ((), ())), preferred_element_type=F32)


def split3(value):
    high = value.astype(BF16).astype(F32)
    middle = (value - high).astype(BF16).astype(F32)
    return high, middle, value - high - middle


def kernel(
    dims,
    movie_h, pieces_h, light_h, mixing_h, owner_ref, offset_ref, traces_ref, ar1_ref, ar2_ref,
    out_ref, bg_ref,
    movie, pieces, light, mixing, load_sems,
    slot_m, slot_j, tile_hot, req_out, req_in, owner_hot,
    both_traces, current, current_b,
    block_gram, piece_movie, piece_light, piece_norm, light_movie,
    ext_out, ext_in, dense_ext, dense_ext_in, counts, counts_b, raw_terms,
    rep_out, rep_in, cop, cop_in, terms, num_row, num_row_in,
    spread, send_out, send_in, num_in, gathered, dense, dense_in,
    send_sems, recv_sems,
):
    X, Y, Z, S = dims
    ZH = Z // 2
    M = X * Y * ZH
    MH = M // 2
    NCH = S // 256
    gx, gy, a = lax.axis_index("gx"), lax.axis_index("gy"), lax.axis_index("ta")
    x, y, z = gx // Y, gx % Y, gy
    sibling = (gx, gy, 1 - a)

    def displacement(m):
        dx = (X // 2 + X - m // (Y * ZH)) % X
        dy = (Y // 2 + Y - (m // ZH) % Y) % Y
        dz = 2 * ((ZH // 2 + ZH - m % ZH) % ZH) + (dx + dy + a) % 2
        return dx, dy, dz

    def to_owner(m):
        dx, dy, dz = displacement(m)
        return ((x + dx) % X) * Y + (y + dy) % Y, (z + dz) % Z, a

    def to_tile(m):
        dx, dy, dz = displacement(m)
        return ((x + X - dx) % X) * Y + (y + Y - dy) % Y, (z + Z - dz) % Z, a

    def slot_at(m):
        dx, dy, dz = displacement(m)
        return (((x + X - dx) % X) * Y + (y + Y - dy) % Y) * ZH + ((z + Z - dz) % Z) // 2

    self_m = (X // 2) * Y * ZH + (Y // 2) * ZH + ZH // 2

    def send(source, target, m, peer, sem):
        mine = jnp.logical_and(a == 0, m == self_m)

        @pl.when(mine)
        def _():
            pltpu.make_async_copy(source, target, recv_sems.at[sem]).start()

        @pl.when(jnp.logical_not(mine))
        def _():
            pltpu.make_async_remote_copy(
                source, target, send_sems.at[sem], recv_sems.at[sem], device_id=peer, device_id_type=MESH
            ).start()

    def wait_in(buffer, sem):
        pltpu.make_async_copy(buffer, buffer, recv_sems.at[sem]).wait()

    def wait_out(buffer, sem):
        @pl.when(a == 0)
        def _():
            part = buffer.at[pl.ds(0, M - 1)]
            pltpu.make_async_copy(part, part, send_sems.at[sem]).wait()

        @pl.when(a == 1)
        def _():
            pltpu.make_async_copy(buffer, buffer, send_sems.at[sem]).wait()

    def to_sibling(source, target, sem):
        copy = pltpu.make_async_remote_copy(
            source, target, send_sems.at[sem], recv_sems.at[sem], device_id=sibling, device_id_type=MESH
        )
        copy.start()
        return copy

    loads = []
    rows = movie.shape[0] // 4
    light_load = pltpu.make_async_copy(light_h, light, load_sems.at[8])
    light_load.start()
    for part in range(4):
        span = pl.ds(part * rows, rows)
        pair = (
            pltpu.make_async_copy(pieces_h.at[span], pieces.at[span], load_sems.at[part]),
            pltpu.make_async_copy(movie_h.at[span], movie.at[span], load_sems.at[4 + part]),
        )
        for copy in pair:
            copy.start()
        loads.append(pair)
    mixing_load = pltpu.make_async_copy(mixing_h, mixing, load_sems.at[9])
    mixing_load.start()

    barrier = pltpu.get_barrier_semaphore()

    def greet(m, carry):
        @pl.when(jnp.logical_not(jnp.logical_and(a == 0, m == self_m)))
        def _():
            pl.semaphore_signal(barrier, inc=1, device_id=to_owner(m), device_id_type=MESH)

        return carry

    pl.semaphore_signal(barrier, inc=1, device_id=sibling, device_id_type=MESH)
    lax.fori_loop(0, M, greet, 0)

    own_of = owner_ref[...]
    far = own_of // Z
    rel_x = (far // Y - x) & (X - 1)
    rel_y = (far % Y - y) & (Y - 1)
    rel_z = (own_of % Z - z) & (Z - 1)
    parity = (rel_x + rel_y + rel_z) & 1
    partner = (
        ((X // 2 - rel_x) & (X - 1)) * (Y * ZH)
        + ((Y // 2 - rel_y) & (Y - 1)) * ZH
        + ((ZH // 2 - (rel_z >> 1)) & (ZH - 1))
    )
    partner = jnp.where(parity == a, partner, -1)
    before = jnp.where(iota((256, 256), 0) < iota((256, 256), 1), 1.0, 0.0).astype(BF16)
    base = jnp.zeros((M, 1), F32)
    asked = jnp.zeros((2 * M, 2 * CAP), F32)
    place1 = offset_ref[...] + 1
    for chunk in range(NCH):
        lanes = slice(chunk * 256, chunk * 256 + 256)
        who = partner[:, lanes]
        match = iota((M, 256), 0) == who
        match_f = jnp.where(match, 1.0, 0.0)
        count = dot(match_f.astype(BF16), before) + base
        rank = jnp.sum(match_f * count, axis=0, keepdims=True).astype(I32)
        base = base + jnp.sum(match_f, axis=1, keepdims=True)
        slot_m[chunk] = who
        slot_j[chunk] = rank
        wanted = place1[:, lanes]
        halves = jnp.concatenate(
            [
                jnp.where(match, (wanted >> 5).astype(F32), 0.0),
                jnp.where(match, (wanted & 31).astype(F32), 0.0),
            ],
            axis=0,
        ).astype(BF16)
        where_to = jnp.where((iota((2 * CAP, 256), 0) & (CAP - 1)) == rank, 1.0, 0.0).astype(BF16)
        asked = asked + dot_t(halves, where_to)
    req_out[...] = ((asked[:M] * 32.0 + asked[M:]).astype(I32) - 1).reshape(M, 1, 2 * CAP)

    pl.semaphore_wait(barrier, M + a)
    both_traces[a] = traces_ref[...]
    trace_copy = to_sibling(both_traces.at[a], both_traces.at[a], 0)

    def ask(m, carry):
        send(req_out.at[m], req_in.at[m], m, to_owner(m), 1)
        return carry

    lax.fori_loop(0, M, ask, 0)

    def tile_maps(chunk, carry):
        who, rank = slot_m[chunk], slot_j[chunk]
        upper = (who >= MH).astype(I32)
        lanes = pl.ds(pl.multiple_of(chunk * 256, 256), 256)
        for half in range(2):
            row = jnp.where(who >= 0, upper * 128 + half * CAP + rank, -1)
            tile_hot[half, :, lanes] = jnp.where(iota((256, 256), 0) == row, 1.0, 0.0).astype(BF16)
        return carry

    lax.fori_loop(0, NCH, tile_maps, 0)

    light_load.wait()
    same_cell = (iota((256, 256), 0) >> 4) == (iota((256, 256), 1) >> 4)
    diagonal = iota((256, 256), 0) == iota((256, 256), 1)
    light_cell = iota((16, 256), 0) == (iota((16, 256), 1) >> 4)
    movie_cell = (iota((256, 16), 0) >> 4) == iota((256, 16), 1)

    def gram(chunk, carry):
        numer, energy = carry
        span = pl.ds(pl.multiple_of(chunk * 256, 256), 256)
        block, frames = pieces[span, :], movie[span, :]
        lit = light[pl.ds(pl.multiple_of(chunk * 16, 16), 16), :]
        cross = jnp.where(same_cell, dot_t(frames, block), 0.0)
        piece_movie[chunk] = jnp.sum(cross.reshape(16, 16, 256), axis=0)
        square = jnp.where(same_cell, dot_t(block, block), 0.0)
        high = square.astype(BF16)
        block_gram[0, chunk] = high
        block_gram[1, chunk] = (square - high.astype(F32)).astype(BF16)
        piece_norm[chunk] = jnp.sum(jnp.where(diagonal, square, 0.0), axis=0, keepdims=True)
        piece_light[chunk] = jnp.sum(jnp.where(light_cell, dot_t(lit, block), 0.0), axis=0, keepdims=True)
        shine = jnp.where(movie_cell, dot_t(frames, lit), 0.0)
        numer = numer + jnp.sum(shine.reshape(16, 16, 16), axis=0)
        lit_f = lit.astype(F32)
        return numer, energy + lit_f * lit_f

    carry = (jnp.zeros((16, 16), F32), jnp.zeros((16, 1024), F32))
    for part in range(4):
        for copy in loads[part]:
            copy.wait()
        carry = lax.fori_loop(part * NCH // 4, (part + 1) * NCH // 4, gram, carry)
    light_movie[...] = jnp.sum(carry[0], axis=1, keepdims=True)
    energy = jnp.sum(jnp.sum(carry[1], axis=1, keepdims=True), axis=0, keepdims=True)

    trace_copy.wait()
    for q in range(4):
        lanes = slice(q * 256, q * 256 + 256)
        for half in range(2):
            part = both_traces[half, :, lanes]
            current[q, half] = part
            current_b[half, q] = part.astype(BF16)
    wait_in(req_in, 1)

    def answer(build, number):
        right = (iota((1, 256), 1) & (2 * CAP - 1)) >= CAP

        def pair(i, carry):
            index = jnp.concatenate([req_in[2 * i], req_in[2 * i + 1]], axis=1)
            lanes = pl.ds(pl.multiple_of(i * 256, 256), 256)
            if build:
                hot = jnp.where(iota((256, 256), 0) == (index & 255), 1.0, 0.0).astype(BF16)
                owner_hot[:, lanes] = hot
            else:
                hot = owner_hot[:, lanes]
            found = dot(current_b[...].reshape(128, 256), hot).reshape(2, 4, 16, 256)
            group = index >> 8
            total = jnp.zeros((16, 256), F32)
            for q in range(4):
                total = total + jnp.where(group == q, jnp.where(right, found[1, q], found[0, q]), 0.0)
            total = total.astype(BF16)
            for side in range(2):
                m = 2 * i + side
                rep_out[number, m] = total[:, side * 128 : side * 128 + 128]
                send(rep_out.at[number, m], rep_in.at[number, m], m, to_tile(m), 2 + number)
            return carry

        lax.fori_loop(0, MH, pair, 0)

    def extras():
        total = jnp.zeros((M, 2 * CAP), F32)
        for chunk in range(NCH):
            who, rank = slot_m[chunk], slot_j[chunk]
            match = iota((M, 256), 0) == who
            for half, value in ((0, piece_norm[chunk]), (1, piece_light[chunk])):
                spot = jnp.where(iota((2 * CAP, 256), 0) == half * CAP + rank, 1.0, 0.0).astype(BF16)
                for piece in split3(value):
                    total = total + dot_t(jnp.where(match, piece, 0.0).astype(BF16), spot)
        ext_out[...] = total.reshape(M, 1, 2 * CAP)

        def post(m, carry):
            send(ext_out.at[m], ext_in.at[m], m, to_owner(m), 4)
            return carry

        lax.fori_loop(0, M, post, 0)

    def collect_extras():
        row, lane = iota((32, 256), 0), iota((32, 256), 1)
        part, group = row >> 3, row & 3
        right = ((lane & (2 * CAP - 1)) >= CAP).astype(I32)
        wanted = jnp.logical_or(
            jnp.logical_and(part < 3, ((row >> 2) & 1) == right),
            jnp.logical_and(part == 3, jnp.logical_and(right == 0, ((row >> 2) & 1) == (lane >> 7))),
        )
        wanted = jnp.where(wanted, group, -2)

        def pair(i, carry):
            index = jnp.concatenate([req_in[2 * i], req_in[2 * i + 1]], axis=1)
            value = jnp.concatenate([ext_in[2 * i], ext_in[2 * i + 1]], axis=1)
            high, middle, low = split3(value)
            picked = jnp.where(part == 0, high, jnp.where(part == 1, middle, jnp.where(part == 2, low, 1.0)))
            keep = wanted == (index >> 8)
            lanes = pl.ds(pl.multiple_of(i * 256, 256), 256)
            found = dot_t(jnp.where(keep, picked, 0.0).astype(BF16), owner_hot[:, lanes])
            counts[slot_at(2 * i)] = found[24:28]
            counts[slot_at(2 * i + 1)] = found[28:32]
            return carry + found

        dense_ext[...] = lax.fori_loop(0, MH, pair, jnp.zeros((32, 256), F32))
        for q in range(4):
            counts_b[q] = counts[:, q, :].astype(BF16)

    pending = []
    for number in range(PASSES):
        answer(number == 0, number)
        if number == 0:
            extras()
        wait_in(rep_in.at[number], 2 + number)

        def pick(half):
            def chunk_of(chunk, carry):
                lanes = pl.ds(pl.multiple_of(chunk * 256, 256), 256)
                low = rep_in[number, :MH].reshape(MH * 16, 128)
                top = rep_in[number, MH:].reshape(MH * 16, 128)
                found = dot(jnp.concatenate([low, top], axis=1), tile_hot[half, :, lanes])
                who = slot_m[chunk]
                who = jnp.where(who >= MH, who - MH, who)
                found = found.reshape(MH, 16, 256)
                kept = jnp.where(iota((MH, 16, 256), 0) == who.reshape(1, 1, 256), found, 0.0)
                cop[number, half, chunk] = jnp.sum(kept, axis=0).astype(BF16)
                return carry

            lax.fori_loop(0, NCH, chunk_of, 0)

        pick(1 - a)
        copy = to_sibling(cop.at[number, 1 - a], cop_in.at[number], 5 + number)
        pick(a)
        copy.wait_recv()
        pending.append(copy)

        def term(chunk, carry):
            copies = cop[number, a, chunk] + cop_in[number, chunk]
            model = dot(copies, block_gram[0, chunk]) + dot(copies, block_gram[1, chunk])
            raw = piece_movie[chunk] - model
            raw_terms[chunk] = raw
            return carry[0] + piece_light[chunk] * copies.astype(F32), carry[1] + raw

        lit, level = lax.fori_loop(0, NCH, term, (jnp.zeros((16, 256), F32), jnp.zeros((16, 256), F32)))
        level = (jnp.sum(level, axis=1, keepdims=True) * (1.0 / S)).astype(BF16).astype(F32)
        for chunk in range(NCH):
            terms[number, a, chunk] = (raw_terms[chunk] - level).astype(BF16)
        copy = to_sibling(terms.at[number, a], terms.at[number, a], 7 + number)
        pending.append(copy)
        numer = light_movie[...] - jnp.sum(lit, axis=1, keepdims=True)
        spot = iota((16, 128), 1) == iota((16, 128), 0) + 16 * a
        level_spot = iota((16, 128), 1) == iota((16, 128), 0) + 16 * a + 64
        numer = jnp.where(spot, numer, jnp.where(level_spot, level, 0.0))
        numer = jnp.sum(numer, axis=0, keepdims=True)
        numer = numer + jnp.where(jnp.logical_and(iota((1, 128), 1) == 32, a == 0), energy, 0.0)
        num_row[number, a] = numer
        row_copy = to_sibling(num_row.at[number, a], num_row.at[number, a], 9 + number)
        pending.append(row_copy)

        def scatter(half):
            def fill(chunk, carry):
                lanes = pl.ds(pl.multiple_of(chunk * 256, 256), 256)
                who = slot_m[chunk]
                who = jnp.where(who >= MH, who - MH, who)
                value = terms[number, half, chunk].astype(F32)
                mask = iota((MH, 16, 256), 0) == who.reshape(1, 1, 256)
                kept = jnp.where(mask, value.reshape(1, 16, 256), 0.0)
                spread[:, lanes] = kept.reshape(MH * 16, 256).astype(BF16)
                return carry

            lax.fori_loop(0, NCH, fill, 0)
            return dot_t(spread[...], tile_hot[half])

        first = scatter(a)
        copy.wait_recv()
        total = (first + scatter(1 - a)).astype(BF16)
        send_out[number, :MH] = total[:, :128].reshape(MH, 16, 128)
        send_out[number, MH:] = total[:, 128:].reshape(MH, 16, 128)
        row_copy.wait_recv()
        num_row_in[number] = num_row[number, 0] + num_row[number, 1]
        tile_parity = (x + y + z) % 2
        tile_slot = tile_parity * M + (x * Y + y) * ZH + z // 2

        def post(m, carry):
            send(send_out.at[number, m], send_in.at[number, m], m, to_owner(m), 11 + number)
            send(num_row_in.at[number], num_in.at[number, tile_slot], m, to_owner(m), 13 + number)
            return carry

        lax.fori_loop(0, M, post, 0)

        if number == 0:
            wait_in(ext_in, 4)
            collect_extras()
            ext_copy = to_sibling(dense_ext, dense_ext_in, 15)
            pending.append(ext_copy)
            mixing_load.wait()

        half_at = ((x + y + z + a) % 2) * M
        mine = num_in.at[number, pl.ds(half_at, M)]
        wait_in(mine, 13 + number)
        num_copy = to_sibling(mine, mine, 16 + number)
        pending.append(num_copy)

        wait_in(send_in.at[number], 11 + number)
        right = (iota((1, 256), 1) & (2 * CAP - 1)) >= CAP

        def gather_rows(i, carry):
            index = jnp.concatenate([req_in[2 * i], req_in[2 * i + 1]], axis=1)
            value = jnp.concatenate([send_in[number, 2 * i], send_in[number, 2 * i + 1]], axis=1).astype(F32)
            group = index >> 8
            lanes = pl.ds(pl.multiple_of(i * 256, 256), 256)
            for half in range(2):
                for q in range(4):
                    keep = jnp.logical_and(group == q, right if half else jnp.logical_not(right))
                    at = (half * 4 + q) * 16
                    gathered[at : at + 16, lanes] = jnp.where(keep, value, 0.0).astype(BF16)
            return carry

        lax.fori_loop(0, MH, gather_rows, 0)
        sums = dot_t(gathered[...], owner_hot[...]).reshape(2, 4, 16, 256)
        levels = jnp.transpose(mine[...].reshape(M, 128))[64:96].astype(BF16)
        for q in range(4):
            dense[number, :, q] = sums[:, q] + dot(levels, counts_b[q]).reshape(2, 16, 256)
        dense_copy = to_sibling(dense.at[number], dense_in.at[number], 18 + number)
        pending.append(dense_copy)
        if number == 0:
            ext_copy.wait_recv()
        num_copy.wait_recv()
        totals = jnp.sum(num_in[number], axis=0)
        light_energy = jnp.sum(jnp.where(iota((1, 128), 1) == 32, totals, 0.0), axis=1, keepdims=True)
        bg_row = totals / (light_energy + 1e-6)
        bg = jnp.sum(jnp.where(iota((32, 128), 1) == iota((32, 128), 0), bg_row, 0.0), axis=1, keepdims=True)
        dense_copy.wait_recv()
        frame = iota((32, 256), 0)

        def back(values, lag):
            return jnp.where(frame >= lag, pltpu.roll(values, lag, 0), 0.0)

        def ahead(values, lag):
            return jnp.where(frame < 32 - lag, pltpu.roll(values, 32 - lag, 0), 0.0)

        for q in range(4):
            lanes = slice(q * 256, q * 256 + 256)
            ext = dense_ext[...] + dense_ext_in[...]
            weight = ext[q : q + 1] + ext[8 + q : 9 + q] + ext[16 + q : 17 + q]
            shine = ext[4 + q : 5 + q] + ext[12 + q : 13 + q] + ext[20 + q : 21 + q]
            summed = (dense[number, :, q] + dense_in[number, :, q]).reshape(32, 256) - bg * shine
            target = current[q].reshape(32, 256) + summed / jnp.maximum(weight, 1.0)
            g1, g2 = ar1_ref[:, lanes], ar2_ref[:, lanes]
            latest = target
            dual = jnp.zeros_like(target)
            for sweep in range(DECONV_ITERS):
                filtered = latest - g1 * back(latest, 1) - g2 * back(latest, 2)
                spikes = jnp.maximum(filtered + dual, 0.0)
                dual = dual + filtered - spikes
                drive = spikes - dual
                drive = target + (drive - g1 * ahead(drive, 1) - g2 * ahead(drive, 2))
                parts = []
                for block in range(4):
                    matrix = mixing[block * 256 : block * 256 + 256, lanes].astype(F32).reshape(8, 32, 256)
                    parts.append(jnp.sum(matrix * drive.reshape(1, 32, 256), axis=1))
                latest = jnp.concatenate(parts, axis=0)
            latest = latest.reshape(2, 16, 256)
            current[q] = latest
            if number < PASSES - 1:
                current_b[:, q] = latest.astype(BF16)
        if number == PASSES - 1:
            for q in range(4):
                out_ref[:, q * 256 : q * 256 + 256] = current[q, a]
            own = iota((32, 128), 0) == iota((32, 128), 1) + 16 * a
            bg_ref[...] = jnp.sum(jnp.where(own, bg, 0.0), axis=0, keepdims=True)

    for copy in pending:
        copy.wait_send()
    wait_out(req_in, 1)
    wait_out(ext_in, 4)
    for number in range(PASSES):
        wait_out(rep_in.at[number], 2 + number)
        wait_out(send_in.at[number], 11 + number)
        wait_out(num_in.at[number, pl.ds(0, M)], 13 + number)


def solution(mesh):
    along_x, Z = mesh.shape["gx"], mesh.shape["gy"]
    X = math.isqrt(along_x)
    Y = along_x // X

    def body(movie, pieces, owner, block_offset, light, traces, ar_first, ar_second, mixing):
        cells, frames, pixels = movie.shape[2], movie.shape[3], movie.shape[4]
        S = cells * pieces.shape[3]
        M = X * Y * Z // 2
        NCH = S // 256
        own = traces.shape[1]
        any_spec = pl.BlockSpec(memory_space=pl.ANY)
        vmem_spec = pl.BlockSpec(memory_space=pltpu.VMEM)
        V = pltpu.VMEM
        scratch = [
            V((cells * frames, pixels), BF16), V((S, pixels), BF16), V((cells, pixels), BF16),
            V((1024, own), BF16), pltpu.SemaphoreType.DMA((10,)),
            V((NCH, 1, 256), I32), V((NCH, 1, 256), I32), V((2, 256, S), BF16),
            V((M, 1, 128), I32), V((M, 1, 128), I32), V((256, M * 128), BF16),
            V((2, 16, own), F32), V((4, 2, 16, 256), F32), V((2, 4, 16, 256), BF16),
            V((2, NCH, 256, 256), BF16), V((NCH, 16, 256), F32), V((NCH, 1, 256), F32),
            V((NCH, 1, 256), F32), V((16, 1), F32),
            V((M, 1, 128), F32), V((M, 1, 128), F32), V((32, 256), F32), V((32, 256), F32),
            V((M, 4, 256), F32), V((4, M, 256), BF16), V((NCH, 16, 256), F32),
            V((PASSES, M, 16, 128), BF16), V((PASSES, M, 16, 128), BF16),
            V((PASSES, 2, NCH, 16, 256), BF16), V((PASSES, NCH, 16, 256), BF16),
            V((PASSES, 2, NCH, 16, 256), BF16),
            V((PASSES, 2, 1, 128), F32), V((PASSES, 1, 128), F32),
            V((M * 8, S), BF16), V((PASSES, M, 16, 128), BF16), V((PASSES, M, 16, 128), BF16),
            V((PASSES, 2 * M, 1, 128), F32), V((128, M * 128), BF16),
            V((PASSES, 2, 4, 16, 256), F32), V((PASSES, 2, 4, 16, 256), F32),
            pltpu.SemaphoreType.DMA((20,)), pltpu.SemaphoreType.DMA((20,)),
        ]
        result, background = pl.pallas_call(
            functools.partial(kernel, (X, Y, Z, S)),
            out_shape=(
                jax.ShapeDtypeStruct((frames, own), F32),
                jax.ShapeDtypeStruct((1, 128), F32),
            ),
            in_specs=[any_spec] * 4 + [vmem_spec] * 5,
            out_specs=(vmem_spec, vmem_spec),
            scratch_shapes=scratch,
            compiler_params=pltpu.CompilerParams(
                collective_id=0, has_side_effects=True, vmem_limit_bytes=56 * 1024 * 1024
            ),
            name="cnmf_passes",
        )(
            movie.reshape(cells * frames, pixels),
            pieces.reshape(S, pixels),
            light.reshape(cells, pixels),
            mixing.reshape(1024, own),
            owner.reshape(1, S),
            block_offset.reshape(1, S),
            traces,
            ar_first.reshape(1, own),
            ar_second.reshape(1, own),
        )
        return result, background[0, :frames]

    in_specs = (
        P("gx", "gy", None, "ta", None),
        P("gx", "gy", None, None, None),
        P("gx", "gy", None, None),
        P("gx", "gy", None),
        P("gx", "gy", None, None),
        P("ta", ("gx", "gy")),
        P(("gx", "gy")),
        P(("gx", "gy")),
        P(None, None, ("gx", "gy")),
    )
    out_specs = (P("ta", ("gx", "gy")), P("ta"))
    return jax.shard_map(body, mesh=mesh, in_specs=in_specs, out_specs=out_specs, check_vma=False)
```

```python
import functools
import math

import jax
import jax.numpy as jnp
from jax import lax
from jax.experimental import pallas as pl
from jax.experimental.pallas import tpu as pltpu
from jax.sharding import PartitionSpec as P

DECONV_ITERS = 3
PASSES = 2
CAP = 64
MESH = pl.DeviceIdType.MESH
F32, BF16, I32 = jnp.float32, jnp.bfloat16, jnp.int32


def iota(shape, axis):
    return lax.broadcasted_iota(I32, shape, axis)


def dot(left, right):
    return lax.dot_general(left, right, (((1,), (0,)), ((), ())), preferred_element_type=F32)


def dot_t(left, right):
    return lax.dot_general(left, right, (((1,), (1,)), ((), ())), preferred_element_type=F32)


def split3(value):
    high = value.astype(BF16).astype(F32)
    middle = (value - high).astype(BF16).astype(F32)
    return high, middle, value - high - middle


def kernel(
    dims,
    movie_h, pieces_h, light_h, mixing_h, owner_ref, offset_ref, traces_ref, ar1_ref, ar2_ref,
    out_ref, bg_ref,
    movie, pieces, light, mixing, load_sems,
    slot_m, slot_j, tile_hot, req_out, req_in, owner_hot, owner_row,
    both_traces, current, current_b,
    block_gram, piece_movie, piece_light, piece_norm, light_movie,
    ext_out, ext_in, dense_ext, dense_ext_in, counts, counts_b, raw_terms,
    rep_out, rep_in, unpacked, cop, cop_in, terms, num_row, num_row_in,
    spread, packed, send_out, send_in, num_in, gathered, dense, dense_in,
    send_sems, recv_sems,
):
    X, Y, Z, S = dims
    ZH = Z // 2
    M = X * Y * ZH
    G = M // 4
    PART = M // 4
    NCH = S // 256
    gx, gy, a = lax.axis_index("gx"), lax.axis_index("gy"), lax.axis_index("ta")
    x, y, z = gx // Y, gx % Y, gy
    sibling = (gx, gy, 1 - a)

    def hops(place):
        dx, dy, half_dz = place
        along_z = sum(min(2 * half_dz + odd, Z - 2 * half_dz - odd) for odd in (0, 1))
        return 2 * min(dx, X - dx) + 2 * min(dy, Y - dy) + along_z

    places = [(i // (Y * ZH), (i // ZH) % Y, i % ZH) for i in range(M)]
    order = sorted(range(M), key=lambda i: (-hops(places[i]), i))
    number_of = [order.index(i) for i in range(M)]
    self_m = number_of[0]

    def displacement(m):
        dx, dy, half_dz = places[order[m]]
        return dx, dy, 2 * half_dz + (dx + dy + a) % 2

    def to_owner(m):
        dx, dy, dz = displacement(m)
        return ((x + dx) % X) * Y + (y + dy) % Y, (z + dz) % Z, a

    def to_tile(m):
        dx, dy, dz = displacement(m)
        return ((x + X - dx) % X) * Y + (y + Y - dy) % Y, (z + Z - dz) % Z, a

    def slot_at(m):
        dx, dy, dz = displacement(m)
        return (((x + X - dx) % X) * Y + (y + Y - dy) % Y) * ZH + ((z + Z - dz) % Z) // 2

    def send(source, target, m, peer, sem, recv=None):
        recv = sem if recv is None else recv
        remote = pltpu.make_async_remote_copy(
            source, target, send_sems.at[sem], recv_sems.at[recv], device_id=peer, device_id_type=MESH
        )
        if m != self_m:
            remote.start()
            return

        @pl.when(a == 0)
        def _():
            pltpu.make_async_copy(source, target, recv_sems.at[recv]).start()

        @pl.when(a == 1)
        def _():
            remote.start()

    left = iota((1, 2 * CAP), 1) < CAP

    def swap_halves(first, second):
        return (
            jnp.where(left, first, pltpu.roll(second, CAP, 1)),
            jnp.where(left, pltpu.roll(first, CAP, 1), second),
        )

    def unpack4(ref, g):
        tiles = [ref[4 * g + side].astype(F32) for side in range(4)]
        low, high = swap_halves(tiles[0], tiles[1]), swap_halves(tiles[2], tiles[3])
        return [jnp.concatenate([low[half], high[half]], axis=1) for half in range(2)]

    def pack4(first, second):
        low = swap_halves(first[:, :128], second[:, :128])
        high = swap_halves(first[:, 128:], second[:, 128:])
        return low + high

    def wait_in(buffer, sem):
        pltpu.make_async_copy(buffer, buffer, recv_sems.at[sem]).wait()

    def wait_out(buffer, sem):
        @pl.when(a == 0)
        def _():
            part = buffer.at[pl.ds(0, M - 1)]
            pltpu.make_async_copy(part, part, send_sems.at[sem]).wait()

        @pl.when(a == 1)
        def _():
            pltpu.make_async_copy(buffer, buffer, send_sems.at[sem]).wait()

    def to_sibling(source, target, sem):
        copy = pltpu.make_async_remote_copy(
            source, target, send_sems.at[sem], recv_sems.at[sem], device_id=sibling, device_id_type=MESH
        )
        copy.start()
        return copy

    loads = []
    rows = movie.shape[0] // 4
    light_load = pltpu.make_async_copy(light_h, light, load_sems.at[8])
    light_load.start()
    for part in range(4):
        span = pl.ds(part * rows, rows)
        pair = (
            pltpu.make_async_copy(pieces_h.at[span], pieces.at[span], load_sems.at[part]),
            pltpu.make_async_copy(movie_h.at[span], movie.at[span], load_sems.at[4 + part]),
        )
        for copy in pair:
            copy.start()
        loads.append(pair)
    mixing_load = pltpu.make_async_copy(mixing_h, mixing, load_sems.at[9])
    mixing_load.start()

    barrier = pltpu.get_barrier_semaphore()

    pl.semaphore_signal(barrier, inc=1, device_id=sibling, device_id_type=MESH)
    for m in range(M):
        if m != self_m:
            pl.semaphore_signal(barrier, inc=1, device_id=to_owner(m), device_id_type=MESH)

    @pl.when(a == 1)
    def _():
        pl.semaphore_signal(barrier, inc=1, device_id=to_owner(self_m), device_id_type=MESH)

    own_of = owner_ref[...]
    far = own_of // Z
    rel_x = (far // Y - x) & (X - 1)
    rel_y = (far % Y - y) & (Y - 1)
    rel_z = (own_of % Z - z) & (Z - 1)
    parity = (rel_x + rel_y + rel_z) & 1
    key = (rel_x * Y + rel_y) * ZH + (rel_z >> 1)
    packed_numbers = jnp.zeros_like(key)
    for word in range(M // 4):
        value = sum(number_of[4 * word + byte] << (8 * byte) for byte in range(4))
        packed_numbers = jnp.where((key >> 2) == word, value, packed_numbers)
    partner = (packed_numbers >> ((key & 3) * 8)) & 255
    partner = jnp.where(parity == a, partner, -1)
    before = jnp.where(iota((256, 256), 0) < iota((256, 256), 1), 1.0, 0.0).astype(BF16)
    base = jnp.zeros((M, 1), F32)
    asked = jnp.zeros((2 * M, 2 * CAP), F32)
    place1 = offset_ref[...] + 1
    for chunk in range(NCH):
        lanes = slice(chunk * 256, chunk * 256 + 256)
        who = partner[:, lanes]
        match = iota((M, 256), 0) == who
        match_f = jnp.where(match, 1.0, 0.0)
        count = dot(match_f.astype(BF16), before) + base
        rank = jnp.sum(match_f * count, axis=0, keepdims=True).astype(I32)
        base = base + jnp.sum(match_f, axis=1, keepdims=True)
        slot_m[chunk] = who
        slot_j[chunk] = rank
        wanted = place1[:, lanes]
        halves = jnp.concatenate(
            [
                jnp.where(match, (wanted >> 5).astype(F32), 0.0),
                jnp.where(match, (wanted & 31).astype(F32), 0.0),
            ],
            axis=0,
        ).astype(BF16)
        where_to = jnp.where((iota((2 * CAP, 256), 0) & (CAP - 1)) == rank, 1.0, 0.0).astype(BF16)
        asked = asked + dot_t(halves, where_to)
    req_out[...] = ((asked[:M] * 32.0 + asked[M:]).astype(I32) - 1).reshape(M, 1, 2 * CAP)

    pl.semaphore_wait(barrier, M + a)
    both_traces[a] = traces_ref[...]
    trace_copy = to_sibling(both_traces.at[a], both_traces.at[a], 0)

    for m in range(M):
        send(req_out.at[m], req_in.at[m], m, to_owner(m), 1)

    def tile_maps(chunk, carry):
        who, rank = slot_m[chunk], slot_j[chunk]
        lanes = pl.ds(pl.multiple_of(chunk * 256, 256), 256)
        row = jnp.where(who >= 0, (who & 3) * CAP + rank, -1)
        tile_hot[:, lanes] = jnp.where(iota((256, 256), 0) == row, 1.0, 0.0).astype(BF16)
        return carry

    lax.fori_loop(0, NCH, tile_maps, 0, unroll=2)

    light_load.wait()
    same_cell = (iota((256, 256), 0) >> 4) == (iota((256, 256), 1) >> 4)
    diagonal = iota((256, 256), 0) == iota((256, 256), 1)
    light_cell = iota((16, 256), 0) == (iota((16, 256), 1) >> 4)
    movie_cell = (iota((256, 16), 0) >> 4) == iota((256, 16), 1)

    def gram(chunk, carry):
        numer, energy = carry
        span = pl.ds(pl.multiple_of(chunk * 256, 256), 256)
        block, frames = pieces[span, :], movie[span, :]
        lit = light[pl.ds(pl.multiple_of(chunk * 16, 16), 16), :]
        cross = jnp.where(same_cell, dot_t(frames, block), 0.0)
        piece_movie[chunk] = jnp.sum(cross.reshape(16, 16, 256), axis=0)
        square = jnp.where(same_cell, dot_t(block, block), 0.0)
        high = square.astype(BF16)
        block_gram[0, chunk] = high
        block_gram[1, chunk] = (square - high.astype(F32)).astype(BF16)
        piece_norm[chunk] = jnp.sum(jnp.where(diagonal, square, 0.0), axis=0, keepdims=True)
        piece_light[chunk] = jnp.sum(jnp.where(light_cell, dot_t(lit, block), 0.0), axis=0, keepdims=True)
        shine = jnp.where(movie_cell, dot_t(frames, lit), 0.0)
        numer = numer + jnp.sum(shine.reshape(16, 16, 16), axis=0)
        lit_f = lit.astype(F32)
        return numer, energy + lit_f * lit_f

    carry = (jnp.zeros((16, 16), F32), jnp.zeros((16, 1024), F32))
    for part in range(4):
        for copy in loads[part]:
            copy.wait()
        carry = lax.fori_loop(part * NCH // 4, (part + 1) * NCH // 4, gram, carry, unroll=2)
    light_movie[...] = jnp.sum(carry[0], axis=1, keepdims=True)
    energy = jnp.sum(jnp.sum(carry[1], axis=1, keepdims=True), axis=0, keepdims=True)

    trace_copy.wait()
    for q in range(4):
        lanes = slice(q * 256, q * 256 + 256)
        for half in range(2):
            part = both_traces[half, :, lanes]
            current[q, half] = part
            current_b[half, q] = part.astype(BF16)
    wait_in(req_in, 1)

    def answer(build, number):
        for g in range(G):
            lanes = slice(g * 256, g * 256 + 256)
            if build:
                asked_for = [req_in[4 * g + side] for side in range(4)]
                index = jnp.concatenate(
                    [jnp.where(left, asked_for[0], asked_for[1]), jnp.where(left, asked_for[2], asked_for[3])], axis=1
                )
                owner_row[g] = index
                hot = jnp.where(iota((256, 256), 0) == (index & 255), 1.0, 0.0).astype(BF16)
                owner_hot[:, lanes] = hot
            else:
                index = owner_row[g]
                hot = owner_hot[:, lanes]
            found = dot(current_b[...].reshape(128, 256), hot).reshape(2, 4, 16, 256)
            block = index >> 8
            totals = [jnp.zeros((16, 256), F32), jnp.zeros((16, 256), F32)]
            for q in range(4):
                keep = block == q
                for half in range(2):
                    totals[half] = totals[half] + jnp.where(keep, found[half, q], 0.0)
            for side, tile in enumerate(pack4(*totals)):
                m = 4 * g + side
                rep_out[number, m] = tile.astype(BF16)
                send(
                    rep_out.at[number, m], rep_in.at[number, m], m, to_tile(m),
                    2 + number, 20 + 4 * number + m // PART,
                )

    def extras():
        total = jnp.zeros((M, 2 * CAP), F32)
        for chunk in range(NCH):
            who, rank = slot_m[chunk], slot_j[chunk]
            match = iota((M, 256), 0) == who
            for half, value in ((0, piece_norm[chunk]), (1, piece_light[chunk])):
                spot = jnp.where(iota((2 * CAP, 256), 0) == half * CAP + rank, 1.0, 0.0).astype(BF16)
                for piece in split3(value):
                    total = total + dot_t(jnp.where(match, piece, 0.0).astype(BF16), spot)
        ext_out[...] = total.reshape(M, 1, 2 * CAP)

        for m in range(M):
            send(ext_out.at[m], ext_in.at[m], m, to_owner(m), 4)

    def collect_extras():
        row, lane = iota((40, 256), 0), iota((40, 256), 1)
        block = row & 3
        second = ((row >> 2) & 1) == 1
        wanted = jnp.where(jnp.logical_or(row < 24, ((row - 24) >> 2) == (lane >> 6)), block, -2)

        total = jnp.zeros((32, 256), F32)
        for g in range(G):
            norms, shines = unpack4(ext_in, g)
            value = jnp.where(second, shines, norms)
            high, middle, low = split3(value)
            picked = jnp.where(row < 8, high, jnp.where(row < 16, middle, jnp.where(row < 24, low, 1.0)))
            keep = wanted == (owner_row[g] >> 8)
            lanes = slice(g * 256, g * 256 + 256)
            found = dot_t(jnp.where(keep, picked, 0.0).astype(BF16), owner_hot[:, lanes])
            for side in range(4):
                counts[slot_at(4 * g + side)] = found[24 + 4 * side : 28 + 4 * side]
            total = total + found[:32]
        dense_ext[...] = total
        for q in range(4):
            counts_b[q] = counts[:, q, :].astype(BF16)

    pending = []
    for number in range(PASSES):
        answer(number == 0, number)
        if number == 0:
            extras()

        def unpack(g, carry):
            for half, block in enumerate(unpack4(rep_in.at[number], g)):
                unpacked[half, g] = block.astype(BF16)
            return carry

        for part in range(4):
            wait_in(rep_in.at[number, pl.ds(part * PART, PART)], 20 + 4 * number + part)
            lax.fori_loop(part * G // 4, (part + 1) * G // 4, unpack, 0, unroll=4)

        def pick(half):
            def chunk_of(chunk, carry):
                lanes = pl.ds(pl.multiple_of(chunk * 256, 256), 256)
                found = dot(unpacked[half].reshape(G * 16, 256), tile_hot[:, lanes]).reshape(G, 16, 256)
                group = slot_m[chunk] >> 2
                kept = jnp.where(iota((G, 16, 256), 0) == group.reshape(1, 1, 256), found, 0.0)
                cop[number, half, chunk] = jnp.sum(kept, axis=0).astype(BF16)
                return carry

            lax.fori_loop(0, NCH, chunk_of, 0, unroll=4)

        pick(1 - a)
        copy = to_sibling(cop.at[number, 1 - a], cop_in.at[number], 5 + number)
        pick(a)
        copy.wait_recv()
        pending.append(copy)

        def term(chunk, carry):
            copies = cop[number, a, chunk] + cop_in[number, chunk]
            model = dot(copies, block_gram[0, chunk]) + dot(copies, block_gram[1, chunk])
            raw = piece_movie[chunk] - model
            raw_terms[chunk] = raw
            return carry[0] + piece_light[chunk] * copies.astype(F32), carry[1] + raw

        lit, level = lax.fori_loop(0, NCH, term, (jnp.zeros((16, 256), F32), jnp.zeros((16, 256), F32)), unroll=4)
        level = (jnp.sum(level, axis=1, keepdims=True) * (1.0 / S)).astype(BF16).astype(F32)
        for chunk in range(NCH):
            terms[number, a, chunk] = (raw_terms[chunk] - level).astype(BF16)
        copy = to_sibling(terms.at[number, a], terms.at[number, a], 7 + number)
        pending.append(copy)
        numer = light_movie[...] - jnp.sum(lit, axis=1, keepdims=True)
        spot = iota((16, 128), 1) == iota((16, 128), 0) + 16 * a
        level_spot = iota((16, 128), 1) == iota((16, 128), 0) + 16 * a + 64
        numer = jnp.where(spot, numer, jnp.where(level_spot, level, 0.0))
        numer = jnp.sum(numer, axis=0, keepdims=True)
        numer = numer + jnp.where(jnp.logical_and(iota((1, 128), 1) == 32, a == 0), energy, 0.0)
        num_row[number, a] = numer
        row_copy = to_sibling(num_row.at[number, a], num_row.at[number, a], 9 + number)
        pending.append(row_copy)

        def scatter(half):
            def fill(chunk, carry):
                lanes = pl.ds(pl.multiple_of(chunk * 256, 256), 256)
                group = slot_m[chunk] >> 2
                value = terms[number, half, chunk].astype(F32)
                mask = iota((G, 16, 256), 0) == group.reshape(1, 1, 256)
                kept = jnp.where(mask, value.reshape(1, 16, 256), 0.0)
                spread[:, lanes] = kept.reshape(G * 16, 256).astype(BF16)
                return carry

            lax.fori_loop(0, NCH, fill, 0, unroll=2)
            packed[half] = dot_t(spread[...], tile_hot[...]).reshape(G, 16, 256)

        scatter(a)
        copy.wait_recv()
        scatter(1 - a)
        row_copy.wait_recv()
        num_row_in[number] = num_row[number, 0] + num_row[number, 1]
        tile_parity = (x + y + z) % 2
        tile_slot = tile_parity * M + (x * Y + y) * ZH + z // 2

        for g in range(G):
            for side, tile in enumerate(pack4(packed[0, g], packed[1, g])):
                m = 4 * g + side
                send_out[number, m] = tile.astype(BF16)
                send(
                    send_out.at[number, m], send_in.at[number, m], m, to_owner(m),
                    11 + number, 28 + 4 * number + m // PART,
                )
        for m in range(M):
            send(num_row_in.at[number], num_in.at[number, tile_slot], m, to_owner(m), 13 + number)

        if number == 0:
            wait_in(ext_in, 4)
            collect_extras()
            ext_copy = to_sibling(dense_ext, dense_ext_in, 15)
            pending.append(ext_copy)
            mixing_load.wait()

        sums = jnp.zeros((128, 256), F32)
        for part in range(4):
            wait_in(send_in.at[number, pl.ds(part * PART, PART)], 28 + 4 * number + part)

            def gather_rows(g, carry):
                block = owner_row[g] >> 8
                lanes = pl.ds(pl.multiple_of(g * 256, 256), 256)
                for half, value in enumerate(unpack4(send_in.at[number], g)):
                    for q in range(4):
                        at = (half * 4 + q) * 16
                        gathered[at : at + 16, lanes] = jnp.where(block == q, value, 0.0).astype(BF16)
                return carry

            lax.fori_loop(part * G // 4, (part + 1) * G // 4, gather_rows, 0, unroll=4)
            lanes = slice(part * PART * CAP, (part + 1) * PART * CAP)
            sums = sums + dot_t(gathered[:, lanes], owner_hot[:, lanes])
        sums = sums.reshape(2, 4, 16, 256)

        half_at = ((x + y + z + a) % 2) * M
        mine = num_in.at[number, pl.ds(half_at, M)]
        wait_in(mine, 13 + number)
        num_copy = to_sibling(mine, mine, 16 + number)
        pending.append(num_copy)
        levels = jnp.transpose(mine[...].reshape(M, 128))[64:96].astype(BF16)
        for q in range(4):
            dense[number, :, q] = sums[:, q] + dot(levels, counts_b[q]).reshape(2, 16, 256)
        dense_copy = to_sibling(dense.at[number], dense_in.at[number], 18 + number)
        pending.append(dense_copy)
        if number == 0:
            ext_copy.wait_recv()
        num_copy.wait_recv()
        totals = jnp.sum(num_in[number], axis=0)
        light_energy = jnp.sum(jnp.where(iota((1, 128), 1) == 32, totals, 0.0), axis=1, keepdims=True)
        bg_row = totals / (light_energy + 1e-6)
        bg = jnp.sum(jnp.where(iota((32, 128), 1) == iota((32, 128), 0), bg_row, 0.0), axis=1, keepdims=True)
        dense_copy.wait_recv()
        frame = iota((32, 256), 0)

        def back(values, lag):
            return jnp.where(frame >= lag, pltpu.roll(values, lag, 0), 0.0)

        def ahead(values, lag):
            return jnp.where(frame < 32 - lag, pltpu.roll(values, 32 - lag, 0), 0.0)

        for q in range(4):
            lanes = slice(q * 256, q * 256 + 256)
            ext = dense_ext[...] + dense_ext_in[...]
            weight = ext[q : q + 1] + ext[8 + q : 9 + q] + ext[16 + q : 17 + q]
            shine = ext[4 + q : 5 + q] + ext[12 + q : 13 + q] + ext[20 + q : 21 + q]
            summed = (dense[number, :, q] + dense_in[number, :, q]).reshape(32, 256) - bg * shine
            target = current[q].reshape(32, 256) + summed / jnp.maximum(weight, 1.0)
            g1, g2 = ar1_ref[:, lanes], ar2_ref[:, lanes]
            latest = target
            dual = jnp.zeros_like(target)
            for sweep in range(DECONV_ITERS):
                filtered = latest - g1 * back(latest, 1) - g2 * back(latest, 2)
                spikes = jnp.maximum(filtered + dual, 0.0)
                dual = dual + filtered - spikes
                drive = spikes - dual
                drive = target + (drive - g1 * ahead(drive, 1) - g2 * ahead(drive, 2))
                parts = []
                for block in range(4):
                    matrix = mixing[block * 256 : block * 256 + 256, lanes].astype(F32).reshape(8, 32, 256)
                    parts.append(jnp.sum(matrix * drive.reshape(1, 32, 256), axis=1))
                latest = jnp.concatenate(parts, axis=0)
            latest = latest.reshape(2, 16, 256)
            current[q] = latest
            if number < PASSES - 1:
                current_b[:, q] = latest.astype(BF16)
        if number == PASSES - 1:
            for q in range(4):
                out_ref[:, q * 256 : q * 256 + 256] = current[q, a]
            own = iota((32, 128), 0) == iota((32, 128), 1) + 16 * a
            bg_ref[...] = jnp.sum(jnp.where(own, bg, 0.0), axis=0, keepdims=True)

    for copy in pending:
        copy.wait_send()
    wait_out(req_in, 1)
    wait_out(ext_in, 4)
    for number in range(PASSES):
        wait_out(rep_in.at[number], 2 + number)
        wait_out(send_in.at[number], 11 + number)
        wait_out(num_in.at[number, pl.ds(0, M)], 13 + number)


def solution(mesh):
    along_x, Z = mesh.shape["gx"], mesh.shape["gy"]
    X = math.isqrt(along_x)
    Y = along_x // X

    def body(movie, pieces, owner, block_offset, light, traces, ar_first, ar_second, mixing):
        cells, frames, pixels = movie.shape[2], movie.shape[3], movie.shape[4]
        S = cells * pieces.shape[3]
        M = X * Y * Z // 2
        NCH = S // 256
        own = traces.shape[1]
        any_spec = pl.BlockSpec(memory_space=pl.ANY)
        vmem_spec = pl.BlockSpec(memory_space=pltpu.VMEM)
        V = pltpu.VMEM
        scratch = [
            V((cells * frames, pixels), BF16), V((S, pixels), BF16), V((cells, pixels), BF16),
            V((1024, own), BF16), pltpu.SemaphoreType.DMA((10,)),
            V((NCH, 1, 256), I32), V((NCH, 1, 256), I32), V((256, S), BF16),
            V((M, 1, 128), I32), V((M, 1, 128), I32), V((256, M * CAP), BF16), V((M // 4, 1, 256), I32),
            V((2, 16, own), F32), V((4, 2, 16, 256), F32), V((2, 4, 16, 256), BF16),
            V((2, NCH, 256, 256), BF16), V((NCH, 16, 256), F32), V((NCH, 1, 256), F32),
            V((NCH, 1, 256), F32), V((16, 1), F32),
            V((M, 1, 128), F32), V((M, 1, 128), F32), V((32, 256), F32), V((32, 256), F32),
            V((M, 4, 256), F32), V((4, M, 256), BF16), V((NCH, 16, 256), F32),
            V((PASSES, M, 16, 128), BF16), V((PASSES, M, 16, 128), BF16), V((2, M // 4, 16, 256), BF16),
            V((PASSES, 2, NCH, 16, 256), BF16), V((PASSES, NCH, 16, 256), BF16),
            V((PASSES, 2, NCH, 16, 256), BF16),
            V((PASSES, 2, 1, 128), F32), V((PASSES, 1, 128), F32),
            V((M * 4, S), BF16), V((2, M // 4, 16, 256), F32), V((PASSES, M, 16, 128), BF16), V((PASSES, M, 16, 128), BF16),
            V((PASSES, 2 * M, 1, 128), F32), V((128, M * CAP), BF16),
            V((PASSES, 2, 4, 16, 256), F32), V((PASSES, 2, 4, 16, 256), F32),
            pltpu.SemaphoreType.DMA((20,)), pltpu.SemaphoreType.DMA((36,)),
        ]
        result, background = pl.pallas_call(
            functools.partial(kernel, (X, Y, Z, S)),
            out_shape=(
                jax.ShapeDtypeStruct((frames, own), F32),
                jax.ShapeDtypeStruct((1, 128), F32),
            ),
            in_specs=[any_spec] * 4 + [vmem_spec] * 5,
            out_specs=(vmem_spec, vmem_spec),
            scratch_shapes=scratch,
            compiler_params=pltpu.CompilerParams(
                collective_id=0, has_side_effects=True, vmem_limit_bytes=56 * 1024 * 1024
            ),
            name="cnmf_passes",
        )(
            movie.reshape(cells * frames, pixels),
            pieces.reshape(S, pixels),
            light.reshape(cells, pixels),
            mixing.reshape(1024, own),
            owner.reshape(1, S),
            block_offset.reshape(1, S),
            traces,
            ar_first.reshape(1, own),
            ar_second.reshape(1, own),
        )
        return result, background[0, :frames]

    in_specs = (
        P("gx", "gy", None, "ta", None),
        P("gx", "gy", None, None, None),
        P("gx", "gy", None, None),
        P("gx", "gy", None),
        P("gx", "gy", None, None),
        P("ta", ("gx", "gy")),
        P(("gx", "gy")),
        P(("gx", "gy")),
        P(None, None, ("gx", "gy")),
    )
    out_specs = (P("ta", ("gx", "gy")), P("ta"))
    return jax.shard_map(body, mesh=mesh, in_specs=in_specs, out_specs=out_specs, check_vma=False)
```

```python
import functools
import math

import jax
import jax.numpy as jnp
from jax import lax
from jax.experimental import pallas as pl
from jax.experimental.pallas import tpu as pltpu
from jax.sharding import PartitionSpec as P

DECONV_ITERS = 3
PASSES = 2
CAP = 64
EARLY = 2
MESH = pl.DeviceIdType.MESH
F32, BF16, I32 = jnp.float32, jnp.bfloat16, jnp.int32


def iota(shape, axis):
    return lax.broadcasted_iota(I32, shape, axis)


def dot(left, right):
    return lax.dot_general(left, right, (((1,), (0,)), ((), ())), preferred_element_type=F32)


def dot_t(left, right):
    return lax.dot_general(left, right, (((1,), (1,)), ((), ())), preferred_element_type=F32)


def split3(value):
    high = value.astype(BF16).astype(F32)
    middle = (value - high).astype(BF16).astype(F32)
    return high, middle, value - high - middle


def kernel(
    dims,
    movie_h, pieces_h, light_h, mixing_h, owner_h, offset_h, traces_h, ar1_h, ar2_h,
    out_ref, bg_ref,
    movie, pieces, light, mixing, owner_ref, offset_ref, ar1_ref, ar2_ref, mixing_wide, mixing_turned, driven, load_sems,
    slot_m, slot_j, tile_hot, req_out, req_in, owner_hot, owner_row,
    both_traces, current, current_b,
    block_gram, piece_movie, piece_light, piece_norm, light_movie,
    ext_out, ext_in, dense_ext, dense_ext_in, counts, counts_b, raw_terms,
    rep_out, rep_in, unpacked, cop, cop_in, terms, num_row, num_row_in,
    spread, packed, send_out, send_in, num_in, gathered, dense, dense_in,
    send_sems, recv_sems,
):
    X, Y, Z, S = dims
    ZH = Z // 2
    M = X * Y * ZH
    G = M // 4
    PART = M // 4
    NCH = S // 256
    gx, gy, a = lax.axis_index("gx"), lax.axis_index("gy"), lax.axis_index("ta")
    x, y, z = gx // Y, gx % Y, gy
    sibling = (gx, gy, 1 - a)

    def hops(place):
        dx, dy, half_dz = place
        along_z = sum(min(2 * half_dz + odd, Z - 2 * half_dz - odd) for odd in (0, 1))
        return 2 * min(dx, X - dx) + 2 * min(dy, Y - dy) + along_z

    places = [(i // (Y * ZH), (i // ZH) % Y, i % ZH) for i in range(M)]
    order = sorted(range(M), key=lambda i: (-hops(places[i]), i))
    number_of = [order.index(i) for i in range(M)]
    self_m = number_of[0]

    def displacement(m):
        dx, dy, half_dz = places[order[m]]
        return dx, dy, 2 * half_dz + (dx + dy + a) % 2

    def to_owner(m):
        dx, dy, dz = displacement(m)
        return ((x + dx) % X) * Y + (y + dy) % Y, (z + dz) % Z, a

    def to_tile(m):
        dx, dy, dz = displacement(m)
        return ((x + X - dx) % X) * Y + (y + Y - dy) % Y, (z + Z - dz) % Z, a

    def slot_at(m):
        dx, dy, dz = displacement(m)
        return (((x + X - dx) % X) * Y + (y + Y - dy) % Y) * ZH + ((z + Z - dz) % Z) // 2

    def send(source, target, m, peer, sem, recv=None):
        recv = sem if recv is None else recv
        remote = pltpu.make_async_remote_copy(
            source, target, send_sems.at[sem], recv_sems.at[recv], device_id=peer, device_id_type=MESH
        )
        if m != self_m:
            remote.start()
            return

        @pl.when(a == 0)
        def _():
            pltpu.make_async_copy(source, target, recv_sems.at[recv]).start()

        @pl.when(a == 1)
        def _():
            remote.start()

    left = iota((1, 2 * CAP), 1) < CAP

    def swap_halves(first, second):
        return (
            jnp.where(left, first, pltpu.roll(second, CAP, 1)),
            jnp.where(left, pltpu.roll(first, CAP, 1), second),
        )

    def unpack4(ref, g):
        tiles = [ref[4 * g + side].astype(F32) for side in range(4)]
        low, high = swap_halves(tiles[0], tiles[1]), swap_halves(tiles[2], tiles[3])
        return [jnp.concatenate([low[half], high[half]], axis=1) for half in range(2)]

    def pack4(first, second):
        low = swap_halves(first[:, :128], second[:, :128])
        high = swap_halves(first[:, 128:], second[:, 128:])
        return low + high

    def wait_in(buffer, sem):
        pltpu.make_async_copy(buffer, buffer, recv_sems.at[sem]).wait()

    def wait_out(buffer, sem):
        @pl.when(a == 0)
        def _():
            part = buffer.at[pl.ds(0, M - 1)]
            pltpu.make_async_copy(part, part, send_sems.at[sem]).wait()

        @pl.when(a == 1)
        def _():
            pltpu.make_async_copy(buffer, buffer, send_sems.at[sem]).wait()

    def to_sibling(source, target, sem, recv=None):
        recv = sem if recv is None else recv
        copy = pltpu.make_async_remote_copy(
            source, target, send_sems.at[sem], recv_sems.at[recv], device_id=sibling, device_id_type=MESH
        )
        copy.start()
        return copy

    barrier = pltpu.get_barrier_semaphore()

    pl.semaphore_signal(barrier, inc=1, device_id=sibling, device_id_type=MESH)
    for m in range(M):
        if m != self_m:
            pl.semaphore_signal(barrier, inc=1, device_id=to_owner(m), device_id_type=MESH)

    @pl.when(a == 1)
    def _():
        pl.semaphore_signal(barrier, inc=1, device_id=to_owner(self_m), device_id_type=MESH)

    index_loads = [
        pltpu.make_async_copy(owner_h, owner_ref, load_sems.at[10]),
        pltpu.make_async_copy(offset_h, offset_ref, load_sems.at[11]),
    ]
    traces_load = pltpu.make_async_copy(traces_h, both_traces.at[a], load_sems.at[12])
    lag_loads = [
        pltpu.make_async_copy(ar1_h, ar1_ref, load_sems.at[13]),
        pltpu.make_async_copy(ar2_h, ar2_ref, load_sems.at[14]),
    ]
    for copy in index_loads + [traces_load]:
        copy.start()
    loads = []
    rows = movie.shape[0] // 4
    light_load = pltpu.make_async_copy(light_h, light, load_sems.at[8])
    light_load.start()
    for part in range(4):
        span = pl.ds(part * rows, rows)
        pair = (
            pltpu.make_async_copy(pieces_h.at[span], pieces.at[span], load_sems.at[part]),
            pltpu.make_async_copy(movie_h.at[span], movie.at[span], load_sems.at[4 + part]),
        )
        for copy in pair:
            copy.start()
        loads.append(pair)
    mixing_load = pltpu.make_async_copy(mixing_h, mixing, load_sems.at[9])
    mixing_load.start()
    for copy in lag_loads:
        copy.start()
    for copy in index_loads:
        copy.wait()

    own_of = owner_ref[...]
    far = own_of // Z
    rel_x = (far // Y - x) & (X - 1)
    rel_y = (far % Y - y) & (Y - 1)
    rel_z = (own_of % Z - z) & (Z - 1)
    parity = (rel_x + rel_y + rel_z) & 1
    key = (rel_x * Y + rel_y) * ZH + (rel_z >> 1)
    packed_numbers = jnp.zeros_like(key)
    for word in range(M // 4):
        value = sum(number_of[4 * word + byte] << (8 * byte) for byte in range(4))
        packed_numbers = jnp.where((key >> 2) == word, value, packed_numbers)
    partner = (packed_numbers >> ((key & 3) * 8)) & 255
    partner = jnp.where(parity == a, partner, -1)
    before = jnp.where(iota((256, 256), 0) < iota((256, 256), 1), 1.0, 0.0).astype(BF16)
    base = jnp.zeros((M, 1), F32)
    asked = jnp.zeros((2 * M, 2 * CAP), F32)
    place1 = offset_ref[...] + 1
    for chunk in range(NCH):
        lanes = slice(chunk * 256, chunk * 256 + 256)
        who = partner[:, lanes]
        match = iota((M, 256), 0) == who
        match_f = jnp.where(match, 1.0, 0.0)
        count = dot(match_f.astype(BF16), before) + base
        rank = jnp.sum(match_f * count, axis=0, keepdims=True).astype(I32)
        base = base + jnp.sum(match_f, axis=1, keepdims=True)
        slot_m[chunk] = who
        slot_j[chunk] = rank
        wanted = place1[:, lanes]
        halves = jnp.concatenate(
            [
                jnp.where(match, (wanted >> 5).astype(F32), 0.0),
                jnp.where(match, (wanted & 31).astype(F32), 0.0),
            ],
            axis=0,
        ).astype(BF16)
        where_to = jnp.where((iota((2 * CAP, 256), 0) & (CAP - 1)) == rank, 1.0, 0.0).astype(BF16)
        asked = asked + dot_t(halves, where_to)
    req_out[...] = ((asked[:M] * 32.0 + asked[M:]).astype(I32) - 1).reshape(M, 1, 2 * CAP)

    light_load.wait()
    same_cell = (iota((256, 256), 0) >> 4) == (iota((256, 256), 1) >> 4)
    diagonal = iota((256, 256), 0) == iota((256, 256), 1)
    light_cell = iota((16, 256), 0) == (iota((16, 256), 1) >> 4)
    movie_cell = (iota((256, 16), 0) >> 4) == iota((256, 16), 1)

    def gram(chunk, carry):
        numer, energy = carry
        span = pl.ds(pl.multiple_of(chunk * 256, 256), 256)
        block, frames = pieces[span, :], movie[span, :]
        lit = light[pl.ds(pl.multiple_of(chunk * 16, 16), 16), :]
        cross = jnp.where(same_cell, dot_t(frames, block), 0.0)
        piece_movie[chunk] = jnp.sum(cross.reshape(16, 16, 256), axis=0)
        square = jnp.where(same_cell, dot_t(block, block), 0.0)
        high = square.astype(BF16)
        block_gram[0, chunk] = high
        block_gram[1, chunk] = (square - high.astype(F32)).astype(BF16)
        piece_norm[chunk] = jnp.sum(jnp.where(diagonal, square, 0.0), axis=0, keepdims=True)
        piece_light[chunk] = jnp.sum(jnp.where(light_cell, dot_t(lit, block), 0.0), axis=0, keepdims=True)
        shine = jnp.where(movie_cell, dot_t(frames, lit), 0.0)
        numer = numer + jnp.sum(shine.reshape(16, 16, 16), axis=0)
        lit_f = lit.astype(F32)
        return numer, energy + lit_f * lit_f

    carry = (jnp.zeros((16, 16), F32), jnp.zeros((16, 1024), F32))

    def gram_part(part, carry):
        for copy in loads[part]:
            copy.wait()
        return lax.fori_loop(part * NCH // 4, (part + 1) * NCH // 4, gram, carry, unroll=2)

    for part in range(EARLY):
        carry = gram_part(part, carry)

    pl.semaphore_wait(barrier, M + a)
    traces_load.wait()
    trace_copy = to_sibling(both_traces.at[a], both_traces.at[a], 0)

    for m in range(M):
        send(req_out.at[m], req_in.at[m], m, to_owner(m), 1, 36 + m // PART)

    def tile_maps(chunk, carry):
        who, rank = slot_m[chunk], slot_j[chunk]
        lanes = pl.ds(pl.multiple_of(chunk * 256, 256), 256)
        row = jnp.where(who >= 0, (who & 3) * CAP + rank, -1)
        tile_hot[:, lanes] = jnp.where(iota((256, 256), 0) == row, 1.0, 0.0).astype(BF16)
        return carry

    lax.fori_loop(0, NCH, tile_maps, 0, unroll=2)

    for part in range(EARLY, 4):
        carry = gram_part(part, carry)
    light_movie[...] = jnp.sum(carry[0], axis=1, keepdims=True)
    energy = jnp.sum(jnp.sum(carry[1], axis=1, keepdims=True), axis=0, keepdims=True)

    trace_copy.wait()
    for q in range(4):
        lanes = slice(q * 256, q * 256 + 256)
        for half in range(2):
            part = both_traces[half, :, lanes]
            current[q, half] = part
            current_b[half, q] = part.astype(BF16)

    def answer(build, number):
        for g in reversed(range(G)) if build else range(G):
            lanes = slice(g * 256, g * 256 + 256)
            if build:
                if (4 * g + 4) % PART == 0:
                    part = (4 * g + 4) // PART - 1
                    wait_in(req_in.at[pl.ds(part * PART, PART)], 36 + part)
                asked_for = [req_in[4 * g + side] for side in range(4)]
                index = jnp.concatenate(
                    [jnp.where(left, asked_for[0], asked_for[1]), jnp.where(left, asked_for[2], asked_for[3])], axis=1
                )
                owner_row[g] = index
                hot = jnp.where(iota((256, 256), 0) == (index & 255), 1.0, 0.0).astype(BF16)
                owner_hot[:, lanes] = hot
            else:
                index = owner_row[g]
                hot = owner_hot[:, lanes]
            found = dot(current_b[...].reshape(128, 256), hot).reshape(2, 4, 16, 256)
            block = index >> 8
            totals = [jnp.zeros((16, 256), F32), jnp.zeros((16, 256), F32)]
            for q in range(4):
                keep = block == q
                for half in range(2):
                    totals[half] = totals[half] + jnp.where(keep, found[half, q], 0.0)
            for side, tile in enumerate(pack4(*totals)):
                m = 4 * g + side
                rep_out[number, m] = tile.astype(BF16)
                send(
                    rep_out.at[number, m], rep_in.at[number, m], m, to_tile(m),
                    2 + number, 20 + 4 * number + m // PART,
                )

    def extras():
        total = jnp.zeros((M, 2 * CAP), F32)
        for chunk in range(NCH):
            who, rank = slot_m[chunk], slot_j[chunk]
            match = iota((M, 256), 0) == who
            for half, value in ((0, piece_norm[chunk]), (1, piece_light[chunk])):
                spot = jnp.where(iota((2 * CAP, 256), 0) == half * CAP + rank, 1.0, 0.0).astype(BF16)
                for piece in split3(value):
                    total = total + dot_t(jnp.where(match, piece, 0.0).astype(BF16), spot)
        ext_out[...] = total.reshape(M, 1, 2 * CAP)

        for m in range(M):
            send(ext_out.at[m], ext_in.at[m], m, to_owner(m), 4)

    def collect_extras():
        row, lane = iota((40, 256), 0), iota((40, 256), 1)
        block = row & 3
        second = ((row >> 2) & 1) == 1
        wanted = jnp.where(jnp.logical_or(row < 24, ((row - 24) >> 2) == (lane >> 6)), block, -2)

        total = jnp.zeros((32, 256), F32)
        for g in range(G):
            norms, shines = unpack4(ext_in, g)
            value = jnp.where(second, shines, norms)
            high, middle, low = split3(value)
            picked = jnp.where(row < 8, high, jnp.where(row < 16, middle, jnp.where(row < 24, low, 1.0)))
            keep = wanted == (owner_row[g] >> 8)
            lanes = slice(g * 256, g * 256 + 256)
            found = dot_t(jnp.where(keep, picked, 0.0).astype(BF16), owner_hot[:, lanes])
            for side in range(4):
                counts[slot_at(4 * g + side)] = found[24 + 4 * side : 28 + 4 * side]
            total = total + found[:32]
        dense_ext[...] = total
        for q in range(4):
            counts_b[q] = counts[:, q, :].astype(BF16)

    def turn_mixing():
        mixing_load.wait()

        def widen(i, carry):
            rows = pl.ds(pl.multiple_of(i * 32, 32), 32)
            wide = mixing[rows, :].astype(F32)
            for part in range(8):
                at = pl.ds(pl.multiple_of(part * 1024 + i * 32, 32), 32)
                mixing_wide[at, :] = wide[:, part * 128 : part * 128 + 128]
            return carry

        lax.fori_loop(0, 32, widen, 0, unroll=2)

        def turn(i, carry):
            for part in range(8):
                lanes = slice(part * 128, part * 128 + 128)
                mixing_turned[pl.ds(pl.multiple_of(i * 32, 32), 32), lanes] = mixing_wide[
                    pl.ds(part * 1024 + i, 32, stride=32), :
                ]
            return carry

        lax.fori_loop(0, 32, turn, 0, unroll=2)

    pending = []
    for number in range(PASSES):
        answer(number == 0, number)
        if number == 0:
            extras()

        def unpack(g, carry):
            for half, block in enumerate(unpack4(rep_in.at[number], g)):
                unpacked[half, g] = block.astype(BF16)
            return carry

        for part in range(4):
            wait_in(rep_in.at[number, pl.ds(part * PART, PART)], 20 + 4 * number + part)
            lax.fori_loop(part * G // 4, (part + 1) * G // 4, unpack, 0, unroll=4)

        def pick(half, first, last):
            def chunk_of(chunk, carry):
                lanes = pl.ds(pl.multiple_of(chunk * 256, 256), 256)
                found = dot(unpacked[half].reshape(G * 16, 256), tile_hot[:, lanes]).reshape(G, 16, 256)
                group = slot_m[chunk] >> 2
                kept = jnp.where(iota((G, 16, 256), 0) == group.reshape(1, 1, 256), found, 0.0)
                cop[number, half, chunk] = jnp.sum(kept, axis=0).astype(BF16)
                return carry

            lax.fori_loop(first, last, chunk_of, 0, unroll=4)

        moved = []
        for part in range(2):
            first, last = part * NCH // 2, (part + 1) * NCH // 2
            pick(1 - a, first, last)
            span = pl.ds(first, last - first)
            moved.append(to_sibling(cop.at[number, 1 - a, span], cop_in.at[number, span], (5, 16)[part] + number))
        pick(a, 0, NCH)
        pending.extend(moved)

        def term(chunk, carry):
            copies = cop[number, a, chunk] + cop_in[number, chunk]
            model = dot(copies, block_gram[0, chunk]) + dot(copies, block_gram[1, chunk])
            raw = piece_movie[chunk] - model
            raw_terms[chunk] = raw
            return carry[0] + piece_light[chunk] * copies.astype(F32), carry[1] + raw

        lit_level = (jnp.zeros((16, 256), F32), jnp.zeros((16, 256), F32))
        for part in range(2):
            moved[part].wait_recv()
            lit_level = lax.fori_loop(part * NCH // 2, (part + 1) * NCH // 2, term, lit_level, unroll=4)
        lit, level = lit_level
        level = (jnp.sum(level, axis=1, keepdims=True) * (1.0 / S)).astype(BF16).astype(F32)
        for chunk in range(NCH):
            terms[number, a, chunk] = (raw_terms[chunk] - level).astype(BF16)
        copy = to_sibling(terms.at[number, a], terms.at[number, a], 7 + number)
        pending.append(copy)
        numer = light_movie[...] - jnp.sum(lit, axis=1, keepdims=True)
        spot = iota((16, 128), 1) == iota((16, 128), 0) + 16 * a
        level_spot = iota((16, 128), 1) == iota((16, 128), 0) + 16 * a + 64
        numer = jnp.where(spot, numer, jnp.where(level_spot, level, 0.0))
        numer = jnp.sum(numer, axis=0, keepdims=True)
        numer = numer + jnp.where(jnp.logical_and(iota((1, 128), 1) == 32, a == 0), energy, 0.0)
        num_row[number, a] = numer
        row_copy = to_sibling(num_row.at[number, a], num_row.at[number, a], 9 + number)
        pending.append(row_copy)

        def scatter(half):
            def fill(chunk, carry):
                lanes = pl.ds(pl.multiple_of(chunk * 256, 256), 256)
                group = slot_m[chunk] >> 2
                value = terms[number, half, chunk].astype(F32)
                mask = iota((G, 16, 256), 0) == group.reshape(1, 1, 256)
                kept = jnp.where(mask, value.reshape(1, 16, 256), 0.0)
                spread[:, lanes] = kept.reshape(G * 16, 256).astype(BF16)
                return carry

            lax.fori_loop(0, NCH, fill, 0, unroll=2)
            packed[half] = dot_t(spread[...], tile_hot[...]).reshape(G, 16, 256)

        scatter(a)
        copy.wait_recv()
        scatter(1 - a)
        row_copy.wait_recv()
        num_row_in[number] = num_row[number, 0] + num_row[number, 1]
        tile_parity = (x + y + z) % 2
        tile_slot = tile_parity * M + (x * Y + y) * ZH + z // 2

        for g in range(G):
            for side, tile in enumerate(pack4(packed[0, g], packed[1, g])):
                m = 4 * g + side
                send_out[number, m] = tile.astype(BF16)
                send(
                    send_out.at[number, m], send_in.at[number, m], m, to_owner(m),
                    11 + number, 28 + 4 * number + m // PART,
                )
                send(num_row_in.at[number], num_in.at[number, tile_slot], m, to_owner(m), 13 + number)

        if number == 0:
            wait_in(ext_in, 4)
            turn_mixing()
            collect_extras()
            ext_copy = to_sibling(dense_ext, dense_ext_in, 15)
            pending.append(ext_copy)
            for copy in lag_loads:
                copy.wait()

        sums = jnp.zeros((128, 256), F32)
        for part in range(4):
            if part == 3:
                half_at = ((x + y + z + a) % 2) * M
                mine = num_in.at[number, pl.ds(half_at, M)]
                wait_in(mine, 13 + number)
                num_copy = to_sibling(mine, mine, 20 + number, 40 + number)
                pending.append(num_copy)
            wait_in(send_in.at[number, pl.ds(part * PART, PART)], 28 + 4 * number + part)

            def gather_rows(g, carry):
                block = owner_row[g] >> 8
                lanes = pl.ds(pl.multiple_of(g * 256, 256), 256)
                for half, value in enumerate(unpack4(send_in.at[number], g)):
                    for q in range(4):
                        at = (half * 4 + q) * 16
                        gathered[at : at + 16, lanes] = jnp.where(block == q, value, 0.0).astype(BF16)
                return carry

            lax.fori_loop(part * G // 4, (part + 1) * G // 4, gather_rows, 0, unroll=4)
            lanes = slice(part * PART * CAP, (part + 1) * PART * CAP)
            sums = sums + dot_t(gathered[:, lanes], owner_hot[:, lanes])
        sums = sums.reshape(2, 4, 16, 256)

        levels = jnp.transpose(mine[...].reshape(M, 128))[64:96].astype(BF16)
        for q in range(4):
            dense[number, :, q] = sums[:, q] + dot(levels, counts_b[q]).reshape(2, 16, 256)
        dense_copy = to_sibling(dense.at[number], dense_in.at[number], 18 + number)
        pending.append(dense_copy)
        if number == 0:
            ext_copy.wait_recv()
        num_copy.wait_recv()
        totals = jnp.sum(num_in[number], axis=0)
        light_energy = jnp.sum(jnp.where(iota((1, 128), 1) == 32, totals, 0.0), axis=1, keepdims=True)
        bg_row = totals / (light_energy + 1e-6)
        bg = jnp.sum(jnp.where(iota((32, 128), 1) == iota((32, 128), 0), bg_row, 0.0), axis=1, keepdims=True)
        dense_copy.wait_recv()
        frame = iota((32, 256), 0)

        def back(values, lag):
            return jnp.where(frame >= lag, pltpu.roll(values, lag, 0), 0.0)

        def ahead(values, lag):
            return jnp.where(frame < 32 - lag, pltpu.roll(values, 32 - lag, 0), 0.0)

        for q in range(4):
            lanes = slice(q * 256, q * 256 + 256)
            ext = dense_ext[...] + dense_ext_in[...]
            weight = ext[q : q + 1] + ext[8 + q : 9 + q] + ext[16 + q : 17 + q]
            shine = ext[4 + q : 5 + q] + ext[12 + q : 13 + q] + ext[20 + q : 21 + q]
            summed = (dense[number, :, q] + dense_in[number, :, q]).reshape(32, 256) - bg * shine
            target = current[q].reshape(32, 256) + summed / jnp.maximum(weight, 1.0)
            g1, g2 = ar1_ref[:, lanes], ar2_ref[:, lanes]
            latest = target
            dual = jnp.zeros_like(target)
            for sweep in range(DECONV_ITERS):
                filtered = latest - g1 * back(latest, 1) - g2 * back(latest, 2)
                spikes = jnp.maximum(filtered + dual, 0.0)
                dual = dual + filtered - spikes
                drive = spikes - dual
                drive = target + (drive - g1 * ahead(drive, 1) - g2 * ahead(drive, 2))
                driven[...] = drive
                last = number == PASSES - 1 and sweep == DECONV_ITERS - 1
                latest = jnp.zeros((16 if last else 32, 256), F32)
                for s in range(32):
                    rows = pl.ds(pl.multiple_of(s * 32 + 16 * a, 16), 16) if last else pl.ds(s * 32, 32)
                    latest = latest + mixing_turned[rows, lanes] * driven[s : s + 1, :]
            if number < PASSES - 1:
                latest = latest.reshape(2, 16, 256)
                current[q] = latest
                current_b[:, q] = latest.astype(BF16)
            else:
                out_ref[:, lanes] = latest
        if number == PASSES - 1:
            own = iota((32, 128), 0) == iota((32, 128), 1) + 16 * a
            bg_ref[...] = jnp.sum(jnp.where(own, bg, 0.0), axis=0, keepdims=True)

    for copy in pending:
        copy.wait_send()
    wait_out(req_in, 1)
    wait_out(ext_in, 4)
    for number in range(PASSES):
        wait_out(rep_in.at[number], 2 + number)
        wait_out(send_in.at[number], 11 + number)
        wait_out(num_in.at[number, pl.ds(0, M)], 13 + number)


def solution(mesh):
    along_x, Z = mesh.shape["gx"], mesh.shape["gy"]
    X = math.isqrt(along_x)
    Y = along_x // X

    def body(movie, pieces, owner, block_offset, light, traces, ar_first, ar_second, mixing):
        cells, frames, pixels = movie.shape[2], movie.shape[3], movie.shape[4]
        S = cells * pieces.shape[3]
        M = X * Y * Z // 2
        NCH = S // 256
        own = traces.shape[1]
        any_spec = pl.BlockSpec(memory_space=pl.ANY)
        vmem_spec = pl.BlockSpec(memory_space=pltpu.VMEM)
        V = pltpu.VMEM
        scratch = [
            V((cells * frames, pixels), BF16), V((S, pixels), BF16), V((cells, pixels), BF16),
            V((1024, own), BF16), V((1, S), I32), V((1, S), I32), V((1, own), F32), V((1, own), F32),
            V((own * 8, 128), F32), V((1024, own), F32), V((32, 256), F32),
            pltpu.SemaphoreType.DMA((15,)),
            V((NCH, 1, 256), I32), V((NCH, 1, 256), I32), V((256, S), BF16),
            V((M, 1, 128), I32), V((M, 1, 128), I32), V((256, M * CAP), BF16), V((M // 4, 1, 256), I32),
            V((2, 16, own), F32), V((4, 2, 16, 256), F32), V((2, 4, 16, 256), BF16),
            V((2, NCH, 256, 256), BF16), V((NCH, 16, 256), F32), V((NCH, 1, 256), F32),
            V((NCH, 1, 256), F32), V((16, 1), F32),
            V((M, 1, 128), F32), V((M, 1, 128), F32), V((32, 256), F32), V((32, 256), F32),
            V((M, 4, 256), F32), V((4, M, 256), BF16), V((NCH, 16, 256), F32),
            V((PASSES, M, 16, 128), BF16), V((PASSES, M, 16, 128), BF16), V((2, M // 4, 16, 256), BF16),
            V((PASSES, 2, NCH, 16, 256), BF16), V((PASSES, NCH, 16, 256), BF16),
            V((PASSES, 2, NCH, 16, 256), BF16),
            V((PASSES, 2, 1, 128), F32), V((PASSES, 1, 128), F32),
            V((M * 4, S), BF16), V((2, M // 4, 16, 256), F32), V((PASSES, M, 16, 128), BF16), V((PASSES, M, 16, 128), BF16),
            V((PASSES, 2 * M, 1, 128), F32), V((128, M * CAP), BF16),
            V((PASSES, 2, 4, 16, 256), F32), V((PASSES, 2, 4, 16, 256), F32),
            pltpu.SemaphoreType.DMA((22,)), pltpu.SemaphoreType.DMA((44,)),
        ]
        result, background = pl.pallas_call(
            functools.partial(kernel, (X, Y, Z, S)),
            out_shape=(
                jax.ShapeDtypeStruct((frames, own), F32),
                jax.ShapeDtypeStruct((1, 128), F32),
            ),
            in_specs=[any_spec] * 9,
            out_specs=(vmem_spec, vmem_spec),
            scratch_shapes=scratch,
            compiler_params=pltpu.CompilerParams(
                collective_id=0, has_side_effects=True, vmem_limit_bytes=56 * 1024 * 1024
            ),
            name="cnmf_passes",
        )(
            movie.reshape(cells * frames, pixels),
            pieces.reshape(S, pixels),
            light.reshape(cells, pixels),
            mixing.reshape(1024, own),
            owner.reshape(1, S),
            block_offset.reshape(1, S),
            traces,
            ar_first.reshape(1, own),
            ar_second.reshape(1, own),
        )
        return result, background[0, :frames]

    in_specs = (
        P("gx", "gy", None, "ta", None),
        P("gx", "gy", None, None, None),
        P("gx", "gy", None, None),
        P("gx", "gy", None),
        P("gx", "gy", None, None),
        P("ta", ("gx", "gy")),
        P(("gx", "gy")),
        P(("gx", "gy")),
        P(None, None, ("gx", "gy")),
    )
    out_specs = (P("ta", ("gx", "gy")), P("ta"))
    return jax.shard_map(body, mesh=mesh, in_specs=in_specs, out_specs=out_specs, check_vma=False)
```

```python
import functools
import math

import jax
import jax.numpy as jnp
from jax import lax
from jax.experimental import pallas as pl
from jax.experimental.pallas import tpu as pltpu
from jax.sharding import PartitionSpec as P

DECONV_ITERS = 3
PASSES = 2
CAP = 64
EARLY = 2
MESH = pl.DeviceIdType.MESH
F32, BF16, I32 = jnp.float32, jnp.bfloat16, jnp.int32


def iota(shape, axis):
    return lax.broadcasted_iota(I32, shape, axis)


def dot(left, right):
    return lax.dot_general(left, right, (((1,), (0,)), ((), ())), preferred_element_type=F32)


def dot_t(left, right):
    return lax.dot_general(left, right, (((1,), (1,)), ((), ())), preferred_element_type=F32)


def split3(value):
    high = value.astype(BF16).astype(F32)
    middle = (value - high).astype(BF16).astype(F32)
    return high, middle, value - high - middle


def kernel(
    dims,
    movie_h, pieces_h, light_h, mixing_h, owner_h, offset_h, traces_h, ar1_h, ar2_h,
    out_ref, bg_ref,
    movie, pieces, light, mixing, owner_ref, offset_ref, ar1_ref, ar2_ref, mixing_wide, mixing_turned, driven, load_sems,
    slot_m, slot_j, tile_hot, req_out, req_in, owner_hot, owner_row,
    both_traces, current, current_b,
    block_gram, piece_movie, piece_light, piece_norm, light_movie,
    ext_out, ext_in, dense_ext, dense_ext_in, counts, counts_b, raw_terms,
    rep_out, rep_in, unpacked, cop, cop_in, terms, num_row, num_row_in,
    spread, packed, send_out, send_in, num_in, gathered, dense, dense_in,
    send_sems, recv_sems,
):
    X, Y, Z, S = dims
    ZH = Z // 2
    M = X * Y * ZH
    G = M // 4
    PART = M // 4
    NCH = S // 256
    gx, gy, a = lax.axis_index("gx"), lax.axis_index("gy"), lax.axis_index("ta")
    x, y, z = gx // Y, gx % Y, gy
    sibling = (gx, gy, 1 - a)

    def hops(place):
        dx, dy, half_dz = place
        along_z = sum(min(2 * half_dz + odd, Z - 2 * half_dz - odd) for odd in (0, 1))
        return 2 * min(dx, X - dx) + 2 * min(dy, Y - dy) + along_z

    places = [(i // (Y * ZH), (i // ZH) % Y, i % ZH) for i in range(M)]
    order = sorted(range(M), key=lambda i: (-hops(places[i]), i))
    number_of = [order.index(i) for i in range(M)]
    self_m = number_of[0]

    odd = [a, 1 - a]
    owner_x = [lax.rem(x + d, X) * Y for d in range(X)]
    owner_y = [lax.rem(y + d, Y) for d in range(Y)]
    owner_z = [[lax.rem(z + 2 * d + bit, Z) for bit in odd] for d in range(ZH)]
    tile_x = [lax.rem(x + X - d, X) * Y for d in range(X)]
    tile_y = [lax.rem(y + Y - d, Y) for d in range(Y)]
    tile_z = [[lax.rem(z + Z - 2 * d - bit, Z) for bit in odd] for d in range(ZH)]

    def to_owner(m):
        dx, dy, half_dz = places[order[m]]
        return owner_x[dx] + owner_y[dy], owner_z[half_dz][(dx + dy) % 2], a

    def to_tile(m):
        dx, dy, half_dz = places[order[m]]
        return tile_x[dx] + tile_y[dy], tile_z[half_dz][(dx + dy) % 2], a

    def slot_at(m):
        dx, dy, half_dz = places[order[m]]
        return (tile_x[dx] + tile_y[dy]) * ZH + lax.div(tile_z[half_dz][(dx + dy) % 2], 2)

    def send(source, target, m, peer, sem, recv=None):
        recv = sem if recv is None else recv
        remote = pltpu.make_async_remote_copy(
            source, target, send_sems.at[sem], recv_sems.at[recv], device_id=peer, device_id_type=MESH
        )
        if m != self_m:
            remote.start()
            return

        @pl.when(a == 0)
        def _():
            pltpu.make_async_copy(source, target, recv_sems.at[recv]).start()

        @pl.when(a == 1)
        def _():
            remote.start()

    left = iota((1, 2 * CAP), 1) < CAP

    def swap_halves(first, second):
        return (
            jnp.where(left, first, pltpu.roll(second, CAP, 1)),
            jnp.where(left, pltpu.roll(first, CAP, 1), second),
        )

    def unpack4(ref, g):
        tiles = [ref[4 * g + side].astype(F32) for side in range(4)]
        low, high = swap_halves(tiles[0], tiles[1]), swap_halves(tiles[2], tiles[3])
        return [jnp.concatenate([low[half], high[half]], axis=1) for half in range(2)]

    def pack4(first, second):
        low = swap_halves(first[:, :128], second[:, :128])
        high = swap_halves(first[:, 128:], second[:, 128:])
        return low + high

    def wait_in(buffer, sem):
        pltpu.make_async_copy(buffer, buffer, recv_sems.at[sem]).wait()

    def wait_out(buffer, sem):
        @pl.when(a == 0)
        def _():
            part = buffer.at[pl.ds(0, M - 1)]
            pltpu.make_async_copy(part, part, send_sems.at[sem]).wait()

        @pl.when(a == 1)
        def _():
            pltpu.make_async_copy(buffer, buffer, send_sems.at[sem]).wait()

    def to_sibling(source, target, sem, recv=None):
        recv = sem if recv is None else recv
        copy = pltpu.make_async_remote_copy(
            source, target, send_sems.at[sem], recv_sems.at[recv], device_id=sibling, device_id_type=MESH
        )
        copy.start()
        return copy

    barrier = pltpu.get_barrier_semaphore()

    pl.semaphore_signal(barrier, inc=1, device_id=sibling, device_id_type=MESH)
    for m in range(M):
        if m != self_m:
            pl.semaphore_signal(barrier, inc=1, device_id=to_owner(m), device_id_type=MESH)

    @pl.when(a == 1)
    def _():
        pl.semaphore_signal(barrier, inc=1, device_id=to_owner(self_m), device_id_type=MESH)

    index_loads = [
        pltpu.make_async_copy(owner_h, owner_ref, load_sems.at[10]),
        pltpu.make_async_copy(offset_h, offset_ref, load_sems.at[11]),
    ]
    traces_load = pltpu.make_async_copy(traces_h, both_traces.at[a], load_sems.at[12])
    lag_loads = [
        pltpu.make_async_copy(ar1_h, ar1_ref, load_sems.at[13]),
        pltpu.make_async_copy(ar2_h, ar2_ref, load_sems.at[14]),
    ]
    for copy in index_loads + [traces_load]:
        copy.start()
    loads = []
    rows = movie.shape[0] // 4
    light_load = pltpu.make_async_copy(light_h, light, load_sems.at[8])
    light_load.start()
    for part in range(4):
        span = pl.ds(part * rows, rows)
        pair = (
            pltpu.make_async_copy(pieces_h.at[span], pieces.at[span], load_sems.at[part]),
            pltpu.make_async_copy(movie_h.at[span], movie.at[span], load_sems.at[4 + part]),
        )
        for copy in pair:
            copy.start()
        loads.append(pair)
    mixing_load = pltpu.make_async_copy(mixing_h, mixing, load_sems.at[9])
    mixing_load.start()
    for copy in lag_loads:
        copy.start()
    for copy in index_loads:
        copy.wait()

    own_of = owner_ref[...]
    far = own_of // Z
    rel_x = (far // Y - x) & (X - 1)
    rel_y = (far % Y - y) & (Y - 1)
    rel_z = (own_of % Z - z) & (Z - 1)
    parity = (rel_x + rel_y + rel_z) & 1
    key = (rel_x * Y + rel_y) * ZH + (rel_z >> 1)
    packed_numbers = jnp.zeros_like(key)
    for word in range(M // 4):
        value = sum(number_of[4 * word + byte] << (8 * byte) for byte in range(4))
        packed_numbers = jnp.where((key >> 2) == word, value, packed_numbers)
    partner = (packed_numbers >> ((key & 3) * 8)) & 255
    partner = jnp.where(parity == a, partner, -1)
    before = jnp.where(iota((256, 256), 0) < iota((256, 256), 1), 1.0, 0.0).astype(BF16)
    base = jnp.zeros((M, 1), F32)
    asked = jnp.zeros((2 * M, 2 * CAP), F32)
    place1 = offset_ref[...] + 1
    for chunk in range(NCH):
        lanes = slice(chunk * 256, chunk * 256 + 256)
        who = partner[:, lanes]
        match = iota((M, 256), 0) == who
        match_f = jnp.where(match, 1.0, 0.0)
        count = dot(match_f.astype(BF16), before) + base
        rank = jnp.sum(match_f * count, axis=0, keepdims=True).astype(I32)
        base = base + jnp.sum(match_f, axis=1, keepdims=True)
        slot_m[chunk] = who
        slot_j[chunk] = rank
        wanted = place1[:, lanes]
        halves = jnp.concatenate(
            [
                jnp.where(match, (wanted >> 5).astype(F32), 0.0),
                jnp.where(match, (wanted & 31).astype(F32), 0.0),
            ],
            axis=0,
        ).astype(BF16)
        where_to = jnp.where((iota((2 * CAP, 256), 0) & (CAP - 1)) == rank, 1.0, 0.0).astype(BF16)
        asked = asked + dot_t(halves, where_to)
    req_out[...] = ((asked[:M] * 32.0 + asked[M:]).astype(I32) - 1).reshape(M, 1, 2 * CAP)

    light_load.wait()
    same_cell = (iota((256, 256), 0) >> 4) == (iota((256, 256), 1) >> 4)
    diagonal = iota((256, 256), 0) == iota((256, 256), 1)
    light_cell = iota((16, 256), 0) == (iota((16, 256), 1) >> 4)
    movie_cell = (iota((256, 16), 0) >> 4) == iota((256, 16), 1)

    def gram(chunk, carry):
        numer, energy = carry
        span = pl.ds(pl.multiple_of(chunk * 256, 256), 256)
        block, frames = pieces[span, :], movie[span, :]
        lit = light[pl.ds(pl.multiple_of(chunk * 16, 16), 16), :]
        cross = jnp.where(same_cell, dot_t(frames, block), 0.0)
        piece_movie[chunk] = jnp.sum(cross.reshape(16, 16, 256), axis=0)
        square = jnp.where(same_cell, dot_t(block, block), 0.0)
        high = square.astype(BF16)
        block_gram[0, chunk] = high
        block_gram[1, chunk] = (square - high.astype(F32)).astype(BF16)
        piece_norm[chunk] = jnp.sum(jnp.where(diagonal, square, 0.0), axis=0, keepdims=True)
        piece_light[chunk] = jnp.sum(jnp.where(light_cell, dot_t(lit, block), 0.0), axis=0, keepdims=True)
        shine = jnp.where(movie_cell, dot_t(frames, lit), 0.0)
        numer = numer + jnp.sum(shine.reshape(16, 16, 16), axis=0)
        lit_f = lit.astype(F32)
        return numer, energy + lit_f * lit_f

    carry = (jnp.zeros((16, 16), F32), jnp.zeros((16, 1024), F32))

    def gram_part(part, carry):
        for copy in loads[part]:
            copy.wait()
        return lax.fori_loop(part * NCH // 4, (part + 1) * NCH // 4, gram, carry, unroll=2)

    for part in range(EARLY):
        carry = gram_part(part, carry)

    pl.semaphore_wait(barrier, M + a)
    traces_load.wait()
    trace_copy = to_sibling(both_traces.at[a], both_traces.at[a], 0)

    for m in range(M):
        send(req_out.at[m], req_in.at[m], m, to_owner(m), 1, 36 + m // PART)

    def tile_maps(chunk, carry):
        who, rank = slot_m[chunk], slot_j[chunk]
        lanes = pl.ds(pl.multiple_of(chunk * 256, 256), 256)
        row = jnp.where(who >= 0, (who & 3) * CAP + rank, -1)
        tile_hot[:, lanes] = jnp.where(iota((256, 256), 0) == row, 1.0, 0.0).astype(BF16)
        return carry

    lax.fori_loop(0, NCH, tile_maps, 0, unroll=4)

    for part in range(EARLY, 4):
        carry = gram_part(part, carry)
    light_movie[...] = jnp.sum(carry[0], axis=1, keepdims=True)
    energy = jnp.sum(jnp.sum(carry[1], axis=1, keepdims=True), axis=0, keepdims=True)

    trace_copy.wait()
    for q in range(4):
        lanes = slice(q * 256, q * 256 + 256)
        for half in range(2):
            part = both_traces[half, :, lanes]
            current[q, half] = part
            current_b[half, q] = part.astype(BF16)

    def answer(build, number):
        for g in range(G):
            lanes = slice(g * 256, g * 256 + 256)
            if build:
                if (4 * g) % PART == 0:
                    part = 4 * g // PART
                    wait_in(req_in.at[pl.ds(part * PART, PART)], 36 + part)
                asked_for = [req_in[4 * g + side] for side in range(4)]
                index = jnp.concatenate(
                    [jnp.where(left, asked_for[0], asked_for[1]), jnp.where(left, asked_for[2], asked_for[3])], axis=1
                )
                owner_row[g] = index
                hot = jnp.where(iota((256, 256), 0) == (index & 255), 1.0, 0.0).astype(BF16)
                owner_hot[:, lanes] = hot
            else:
                index = owner_row[g]
                hot = owner_hot[:, lanes]
            found = dot(current_b[...].reshape(128, 256), hot).reshape(2, 4, 16, 256)
            block = index >> 8
            totals = [jnp.zeros((16, 256), F32), jnp.zeros((16, 256), F32)]
            for q in range(4):
                keep = block == q
                for half in range(2):
                    totals[half] = totals[half] + jnp.where(keep, found[half, q], 0.0)
            for side, tile in enumerate(pack4(*totals)):
                m = 4 * g + side
                rep_out[number, m] = tile.astype(BF16)
                send(
                    rep_out.at[number, m], rep_in.at[number, m], m, to_tile(m),
                    2 + number, 20 + 4 * number + m // PART,
                )

    def extras():
        total = jnp.zeros((M, 2 * CAP), F32)
        for chunk in range(NCH):
            who, rank = slot_m[chunk], slot_j[chunk]
            match = iota((M, 256), 0) == who
            for half, value in ((0, piece_norm[chunk]), (1, piece_light[chunk])):
                spot = jnp.where(iota((2 * CAP, 256), 0) == half * CAP + rank, 1.0, 0.0).astype(BF16)
                for piece in split3(value):
                    total = total + dot_t(jnp.where(match, piece, 0.0).astype(BF16), spot)
        ext_out[...] = total.reshape(M, 1, 2 * CAP)

        for m in range(M):
            send(ext_out.at[m], ext_in.at[m], m, to_owner(m), 4)

    def collect_extras():
        row, lane = iota((40, 256), 0), iota((40, 256), 1)
        block = row & 3
        second = ((row >> 2) & 1) == 1
        wanted = jnp.where(jnp.logical_or(row < 24, ((row - 24) >> 2) == (lane >> 6)), block, -2)

        total = jnp.zeros((32, 256), F32)
        for g in range(G):
            norms, shines = unpack4(ext_in, g)
            value = jnp.where(second, shines, norms)
            high, middle, low = split3(value)
            picked = jnp.where(row < 8, high, jnp.where(row < 16, middle, jnp.where(row < 24, low, 1.0)))
            keep = wanted == (owner_row[g] >> 8)
            lanes = slice(g * 256, g * 256 + 256)
            found = dot_t(jnp.where(keep, picked, 0.0).astype(BF16), owner_hot[:, lanes])
            for side in range(4):
                counts[slot_at(4 * g + side)] = found[24 + 4 * side : 28 + 4 * side]
            total = total + found[:32]
        dense_ext[...] = total
        for q in range(4):
            counts_b[q] = counts[:, q, :].astype(BF16)

    def turn_mixing():
        mixing_load.wait()

        def widen(i, carry):
            rows = pl.ds(pl.multiple_of(i * 32, 32), 32)
            wide = mixing[rows, :].astype(F32)
            for part in range(8):
                at = pl.ds(pl.multiple_of(part * 1024 + i * 32, 32), 32)
                mixing_wide[at, :] = wide[:, part * 128 : part * 128 + 128]
            return carry

        lax.fori_loop(0, 32, widen, 0, unroll=2)

        def turn(i, carry):
            for part in range(8):
                lanes = slice(part * 128, part * 128 + 128)
                mixing_turned[pl.ds(pl.multiple_of(i * 32, 32), 32), lanes] = mixing_wide[
                    pl.ds(part * 1024 + i, 32, stride=32), :
                ]
            return carry

        lax.fori_loop(0, 32, turn, 0, unroll=2)

    pending = []
    for number in range(PASSES):
        if number == 0:
            extras()
        answer(number == 0, number)

        def unpack(g, carry):
            for half, block in enumerate(unpack4(rep_in.at[number], g)):
                unpacked[half, g] = block.astype(BF16)
            return carry

        for part in range(4):
            wait_in(rep_in.at[number, pl.ds(part * PART, PART)], 20 + 4 * number + part)
            lax.fori_loop(part * G // 4, (part + 1) * G // 4, unpack, 0, unroll=4)

        def pick(half, first, last):
            def chunk_of(chunk, carry):
                lanes = pl.ds(pl.multiple_of(chunk * 256, 256), 256)
                found = dot(unpacked[half].reshape(G * 16, 256), tile_hot[:, lanes]).reshape(G, 16, 256)
                group = slot_m[chunk] >> 2
                kept = jnp.where(iota((G, 16, 256), 0) == group.reshape(1, 1, 256), found, 0.0)
                cop[number, half, chunk] = jnp.sum(kept, axis=0).astype(BF16)
                return carry

            lax.fori_loop(first, last, chunk_of, 0, unroll=4)

        moved = []
        for part in range(2):
            first, last = part * NCH // 2, (part + 1) * NCH // 2
            pick(1 - a, first, last)
            span = pl.ds(first, last - first)
            moved.append(to_sibling(cop.at[number, 1 - a, span], cop_in.at[number, span], (5, 16)[part] + number))
        pick(a, 0, NCH)
        pending.extend(moved)

        def term(chunk, carry):
            copies = cop[number, a, chunk] + cop_in[number, chunk]
            model = dot(copies, block_gram[0, chunk]) + dot(copies, block_gram[1, chunk])
            raw = piece_movie[chunk] - model
            raw_terms[chunk] = raw
            return carry[0] + piece_light[chunk] * copies.astype(F32), carry[1] + raw

        lit_level = (jnp.zeros((16, 256), F32), jnp.zeros((16, 256), F32))
        for part in range(2):
            moved[part].wait_recv()
            lit_level = lax.fori_loop(part * NCH // 2, (part + 1) * NCH // 2, term, lit_level, unroll=4)
        lit, level = lit_level
        level = (jnp.sum(level, axis=1, keepdims=True) * (1.0 / S)).astype(BF16).astype(F32)
        for chunk in range(NCH):
            terms[number, a, chunk] = (raw_terms[chunk] - level).astype(BF16)
        copy = to_sibling(terms.at[number, a], terms.at[number, a], 7 + number)
        pending.append(copy)
        numer = light_movie[...] - jnp.sum(lit, axis=1, keepdims=True)
        spot = iota((16, 128), 1) == iota((16, 128), 0) + 16 * a
        level_spot = iota((16, 128), 1) == iota((16, 128), 0) + 16 * a + 64
        numer = jnp.where(spot, numer, jnp.where(level_spot, level, 0.0))
        numer = jnp.sum(numer, axis=0, keepdims=True)
        numer = numer + jnp.where(jnp.logical_and(iota((1, 128), 1) == 32, a == 0), energy, 0.0)
        num_row[number, a] = numer
        row_copy = to_sibling(num_row.at[number, a], num_row.at[number, a], 9 + number)
        pending.append(row_copy)

        def scatter(half):
            def fill(chunk, carry):
                lanes = pl.ds(pl.multiple_of(chunk * 256, 256), 256)
                group = slot_m[chunk] >> 2
                value = terms[number, half, chunk].astype(F32)
                mask = iota((G, 16, 256), 0) == group.reshape(1, 1, 256)
                kept = jnp.where(mask, value.reshape(1, 16, 256), 0.0)
                spread[:, lanes] = kept.reshape(G * 16, 256).astype(BF16)
                return carry

            lax.fori_loop(0, NCH, fill, 0, unroll=8)
            packed[half] = dot_t(spread[...], tile_hot[...]).reshape(G, 16, 256)

        scatter(a)
        copy.wait_recv()
        scatter(1 - a)
        row_copy.wait_recv()
        num_row_in[number] = num_row[number, 0] + num_row[number, 1]
        tile_parity = (x + y + z) % 2
        tile_slot = tile_parity * M + (x * Y + y) * ZH + z // 2

        for g in range(G):
            for side, tile in enumerate(pack4(packed[0, g], packed[1, g])):
                m = 4 * g + side
                send_out[number, m] = tile.astype(BF16)
                send(
                    send_out.at[number, m], send_in.at[number, m], m, to_owner(m),
                    11 + number, 28 + 4 * number + m // PART,
                )
                send(num_row_in.at[number], num_in.at[number, tile_slot], m, to_owner(m), 13 + number)

        if number == 0:
            wait_in(ext_in, 4)
            turn_mixing()
            collect_extras()
            ext_copy = to_sibling(dense_ext, dense_ext_in, 15)
            pending.append(ext_copy)
            for copy in lag_loads:
                copy.wait()

        sums = jnp.zeros((128, 256), F32)
        for part in range(4):
            if part == 3:
                half_at = ((x + y + z + a) % 2) * M
                mine = num_in.at[number, pl.ds(half_at, M)]
                wait_in(mine, 13 + number)
                num_copy = to_sibling(mine, mine, 20 + number, 40 + number)
                pending.append(num_copy)
            wait_in(send_in.at[number, pl.ds(part * PART, PART)], 28 + 4 * number + part)

            def gather_rows(g, carry):
                block = owner_row[g] >> 8
                lanes = pl.ds(pl.multiple_of(g * 256, 256), 256)
                for half, value in enumerate(unpack4(send_in.at[number], g)):
                    for q in range(4):
                        at = (half * 4 + q) * 16
                        gathered[at : at + 16, lanes] = jnp.where(block == q, value, 0.0).astype(BF16)
                return carry

            lax.fori_loop(part * G // 4, (part + 1) * G // 4, gather_rows, 0, unroll=4)
            lanes = slice(part * PART * CAP, (part + 1) * PART * CAP)
            sums = sums + dot_t(gathered[:, lanes], owner_hot[:, lanes])
        sums = sums.reshape(2, 4, 16, 256)

        levels = jnp.transpose(mine[...].reshape(M, 128))[64:96].astype(BF16)
        for q in range(4):
            dense[number, :, q] = sums[:, q] + dot(levels, counts_b[q]).reshape(2, 16, 256)
        dense_copy = to_sibling(dense.at[number], dense_in.at[number], 18 + number)
        pending.append(dense_copy)
        if number == 0:
            ext_copy.wait_recv()
        num_copy.wait_recv()
        totals = jnp.sum(num_in[number], axis=0)
        light_energy = jnp.sum(jnp.where(iota((1, 128), 1) == 32, totals, 0.0), axis=1, keepdims=True)
        bg_row = totals / (light_energy + 1e-6)
        bg = jnp.sum(jnp.where(iota((32, 128), 1) == iota((32, 128), 0), bg_row, 0.0), axis=1, keepdims=True)
        dense_copy.wait_recv()
        frame = iota((32, 256), 0)

        def back(values, lag):
            return jnp.where(frame >= lag, pltpu.roll(values, lag, 0), 0.0)

        def ahead(values, lag):
            return jnp.where(frame < 32 - lag, pltpu.roll(values, 32 - lag, 0), 0.0)

        for pair in range(2):
            states = []
            for q in (2 * pair, 2 * pair + 1):
                lanes = slice(q * 256, q * 256 + 256)
                ext = dense_ext[...] + dense_ext_in[...]
                weight = ext[q : q + 1] + ext[8 + q : 9 + q] + ext[16 + q : 17 + q]
                shine = ext[4 + q : 5 + q] + ext[12 + q : 13 + q] + ext[20 + q : 21 + q]
                summed = (dense[number, :, q] + dense_in[number, :, q]).reshape(32, 256) - bg * shine
                target = current[q].reshape(32, 256) + summed / jnp.maximum(weight, 1.0)
                states.append([q, lanes, target, target, jnp.zeros_like(target)])
            for sweep in range(DECONV_ITERS):
                last = number == PASSES - 1 and sweep == DECONV_ITERS - 1
                for state in states:
                    q, lanes, target, latest, dual = state
                    g1, g2 = ar1_ref[:, lanes], ar2_ref[:, lanes]
                    filtered = latest - g1 * back(latest, 1) - g2 * back(latest, 2)
                    spikes = jnp.maximum(filtered + dual, 0.0)
                    dual = dual + filtered - spikes
                    drive = spikes - dual
                    driven[q * DECONV_ITERS + sweep] = target + (drive - g1 * ahead(drive, 1) - g2 * ahead(drive, 2))
                    state[4] = dual
                for state in states:
                    q, lanes = state[:2]
                    latest = jnp.zeros((16 if last else 32, 256), F32)
                    for s in range(32):
                        rows = pl.ds(pl.multiple_of(s * 32 + 16 * a, 16), 16) if last else pl.ds(s * 32, 32)
                        latest = latest + mixing_turned[rows, lanes] * driven[q * DECONV_ITERS + sweep, s : s + 1, :]
                    state[3] = latest
            for q, lanes, target, latest, dual in states:
                if number < PASSES - 1:
                    latest = latest.reshape(2, 16, 256)
                    current[q] = latest
                    current_b[:, q] = latest.astype(BF16)
                else:
                    out_ref[:, lanes] = latest
        if number == PASSES - 1:
            own = iota((32, 128), 0) == iota((32, 128), 1) + 16 * a
            bg_ref[...] = jnp.sum(jnp.where(own, bg, 0.0), axis=0, keepdims=True)

    for copy in pending:
        copy.wait_send()
    wait_out(req_in, 1)
    wait_out(ext_in, 4)
    for number in range(PASSES):
        wait_out(rep_in.at[number], 2 + number)
        wait_out(send_in.at[number], 11 + number)
        wait_out(num_in.at[number, pl.ds(0, M)], 13 + number)


def solution(mesh):
    along_x, Z = mesh.shape["gx"], mesh.shape["gy"]
    X = math.isqrt(along_x)
    Y = along_x // X

    def body(movie, pieces, owner, block_offset, light, traces, ar_first, ar_second, mixing):
        cells, frames, pixels = movie.shape[2], movie.shape[3], movie.shape[4]
        S = cells * pieces.shape[3]
        M = X * Y * Z // 2
        NCH = S // 256
        own = traces.shape[1]
        any_spec = pl.BlockSpec(memory_space=pl.ANY)
        vmem_spec = pl.BlockSpec(memory_space=pltpu.VMEM)
        V = pltpu.VMEM
        scratch = [
            V((cells * frames, pixels), BF16), V((S, pixels), BF16), V((cells, pixels), BF16),
            V((1024, own), BF16), V((1, S), I32), V((1, S), I32), V((1, own), F32), V((1, own), F32),
            V((own * 8, 128), F32), V((1024, own), F32), V((4 * DECONV_ITERS, 32, 256), F32),
            pltpu.SemaphoreType.DMA((15,)),
            V((NCH, 1, 256), I32), V((NCH, 1, 256), I32), V((256, S), BF16),
            V((M, 1, 128), I32), V((M, 1, 128), I32), V((256, M * CAP), BF16), V((M // 4, 1, 256), I32),
            V((2, 16, own), F32), V((4, 2, 16, 256), F32), V((2, 4, 16, 256), BF16),
            V((2, NCH, 256, 256), BF16), V((NCH, 16, 256), F32), V((NCH, 1, 256), F32),
            V((NCH, 1, 256), F32), V((16, 1), F32),
            V((M, 1, 128), F32), V((M, 1, 128), F32), V((32, 256), F32), V((32, 256), F32),
            V((M, 4, 256), F32), V((4, M, 256), BF16), V((NCH, 16, 256), F32),
            V((PASSES, M, 16, 128), BF16), V((PASSES, M, 16, 128), BF16), V((2, M // 4, 16, 256), BF16),
            V((PASSES, 2, NCH, 16, 256), BF16), V((PASSES, NCH, 16, 256), BF16),
            V((PASSES, 2, NCH, 16, 256), BF16),
            V((PASSES, 2, 1, 128), F32), V((PASSES, 1, 128), F32),
            V((M * 4, S), BF16), V((2, M // 4, 16, 256), F32), V((PASSES, M, 16, 128), BF16), V((PASSES, M, 16, 128), BF16),
            V((PASSES, 2 * M, 1, 128), F32), V((128, M * CAP), BF16),
            V((PASSES, 2, 4, 16, 256), F32), V((PASSES, 2, 4, 16, 256), F32),
            pltpu.SemaphoreType.DMA((22,)), pltpu.SemaphoreType.DMA((44,)),
        ]
        result, background = pl.pallas_call(
            functools.partial(kernel, (X, Y, Z, S)),
            out_shape=(
                jax.ShapeDtypeStruct((frames, own), F32),
                jax.ShapeDtypeStruct((1, 128), F32),
            ),
            in_specs=[any_spec] * 9,
            out_specs=(vmem_spec, vmem_spec),
            scratch_shapes=scratch,
            compiler_params=pltpu.CompilerParams(
                collective_id=0, has_side_effects=True, vmem_limit_bytes=56 * 1024 * 1024
            ),
            name="cnmf_passes",
        )(
            movie.reshape(cells * frames, pixels),
            pieces.reshape(S, pixels),
            light.reshape(cells, pixels),
            mixing.reshape(1024, own),
            owner.reshape(1, S),
            block_offset.reshape(1, S),
            traces,
            ar_first.reshape(1, own),
            ar_second.reshape(1, own),
        )
        return result, background[0, :frames]

    in_specs = (
        P("gx", "gy", None, "ta", None),
        P("gx", "gy", None, None, None),
        P("gx", "gy", None, None),
        P("gx", "gy", None),
        P("gx", "gy", None, None),
        P("ta", ("gx", "gy")),
        P(("gx", "gy")),
        P(("gx", "gy")),
        P(None, None, ("gx", "gy")),
    )
    out_specs = (P("ta", ("gx", "gy")), P("ta"))
    return jax.shard_map(body, mesh=mesh, in_specs=in_specs, out_specs=out_specs, check_vma=False)
```
